768 devices in a mesh: orb: 96 (over y, x, z_lo), dom: 8 (over z_hi, core).
Axes of the slice: x: 4, y: 8, z: 12 (z_hi: 4, z_lo: 3; z = z_hi * 3 + z_lo), core: 2. Of those that a mesh axis runs over, the one named last changes fastest.
Arguments:
- orbitals: float32 [2, 96, 32, 96, 128], P(None, 'orb', 'dom'), may hold values from -20 to 20
- potential: float32 [32, 96, 128], P('dom'), may hold values from -1.5 to 0.5
- laser_field: float32 [3], replicated, may hold values from -0.1 to 0.1
- box_anchor: int32 [3, 128], replicated, may hold values from 0 to 120, as said below
- domain_atoms: int32 [8, 32], replicated, may hold values from -1 to 127, as said below
- projector: float32 [4, 512], replicated, may hold values from -0.25 to 0.25
- strength: float32 [4], replicated, may hold values from 4 to 16
Outputs:
- evolved: float32 [2, 96, 32, 96, 128], P(None, 'orb', 'dom')
- density: float32 [32, 96, 128], P('dom', 'orb')
- current: float32 [3, 32, 96, 128], P(None, 'dom', 'orb')
The draws below stay inside these ranges and needn't reach their ends.
Inputs may be any that keep to these rules, and one draw needn't show every extreme that they name: `box_anchor`: column a holds atom a's box corner relative to its domain: the first entry is 0 to 0, the second 0 to 88, the third 0 to 120; some atom has all three at their largest. `domain_atoms`: every atom stands in exactly one row; a row's atoms come first and the rest of the row is -1; a row holds at most 32 atoms and some row exactly 32.
All inputs are finite; a program needn't handle non-finite values.
Results may differ from the reference program's by a relative error of at most 0.0001.
Values sent between devices are 32-bit elements; how exact they have to be, the bound alone decides.
No kernel may reach another device: no remote copies, remote signals or barrier semaphores. Data moves between devices by JAX's collectives and lax.ppermute only.
A program may use at most 64 MiB of HBM per device.

```python
import math
import jax
import jax.numpy as jnp
from jax import lax

SX = 4
NZ = 128
APD = 16
TERMS = 4
BOX = 8
PROJ = 4
ORBITALS = 96
NX = 32
NY = 96
ATOMS = 128
CAP = 32
N_DOM = 8


def draw_box_anchor(key, part):
    key = jax.random.fold_in(key, 11)
    keys = jax.random.split(key, 4)
    along_x = jax.random.randint(keys[0], (ATOMS,), 0, SX - 3)
    along_y = jax.random.randint(keys[1], (ATOMS,), 0, NY - BOX + 1)
    along_z = jax.random.randint(keys[2], (ATOMS,), 0, NZ - BOX + 1)
    chosen = jax.random.randint(keys[3], (), 0, ATOMS)
    along_x = along_x.at[chosen].set(SX - 4)
    along_y = along_y.at[chosen].set(NY - BOX)
    along_z = along_z.at[chosen].set(NZ - BOX)
    return jnp.stack([along_x, along_y, along_z]).astype(jnp.int32)


def draw_domain_atoms(key, part):
    key = jax.random.fold_in(key, 23)
    keys = jax.random.split(key, 2)
    quarter = N_DOM // 4
    ranking = jax.random.permutation(keys[0], N_DOM).astype(jnp.int32)
    profile = jnp.array([2 * APD, APD + APD // 2, APD // 2, 0], jnp.int32)
    counts = profile[ranking // quarter]
    row_ends = jnp.cumsum(counts).astype(jnp.int32)
    row_starts = row_ends - counts
    shuffled = jax.random.permutation(keys[1], ATOMS).astype(jnp.int32)
    slot_ids = jnp.arange(CAP, dtype=jnp.int32)
    position = jnp.minimum(row_starts[:, None] + slot_ids[None, :], ATOMS - 1)
    return jnp.where(slot_ids[None, :] < counts[:, None], shuffled[position], -1).astype(jnp.int32)


def strengthened(result, key, source, target, parts, factor):
    owner, partner = [(jnp.arange(result.shape[dim]) // (result.shape[dim] // parts)).reshape([-1 if axis == dim else 1 for axis in range(result.ndim)]) for dim in (source, target)]
    chosen = jax.random.permutation(key, parts)[partner]
    strong = (owner == chosen) | (owner == (partner + parts // 2) % parts)
    return jnp.where(strong, factor * result, result)


def block_levels(key, extent, shards, low, largest):
    def one(axis_at, blocks):
        draws = jax.random.uniform(jax.random.fold_in(jax.random.fold_in(key, 6), axis_at), (blocks,), jnp.float32, low / len(shards), largest / len(shards))
        return jnp.repeat(jnp.exp(draws), extent[axis_at] // blocks).reshape((-1,) + (1,) * (len(extent) - axis_at - 1))

    factor_of = one(*shards[0])
    for cut in shards[1:]:
        factor_of = factor_of * one(*cut)
    return factor_of


def gaussian(rng, dims, scale, reach, cuts=(), kind=jnp.bfloat16):
    gain = block_levels(rng, dims, cuts, -0.22, 0.18) if cuts else 1.0
    values = jax.random.normal(rng, dims, jnp.float32) * scale * gain
    return jnp.minimum(jnp.maximum(values, -reach), reach).astype(kind)


def gaussian_with(own_key, extent, deviation, limit, shards, heavy, kind=jnp.bfloat16):
    drawn = deviation * jax.random.normal(own_key, extent, jnp.float32)
    if shards:
        drawn = drawn * block_levels(own_key, extent, shards, -0.22, 0.18)
    return jnp.clip(strengthened(drawn, jax.random.fold_in(own_key, 3), *heavy), -limit, limit).astype(kind)


def setup_inputs(seed: int = 0) -> dict:
    seeds = jax.random.split(jax.random.key(seed), 8)
    return {
        "orbitals": gaussian_with(seeds[0], (2, ORBITALS, NX, NY, NZ), 1.0, 20.0, ((1, 96), (2, 8)), (1, 3, 96, 4.75), jnp.float32),
        "potential": jnp.clip(-1.5 + 2.0 * jax.random.uniform(seeds[1], (NX, NY, NZ), jnp.float32) ** block_levels(seeds[1], (NX, NY, NZ), ((0, 8),), -0.2, 0.2), -1.5, 0.5),
        "laser_field": jnp.clip(jax.random.uniform(seeds[2], (3,), jnp.float32, -0.1, 0.1), -0.1, 0.1),
        "box_anchor": draw_box_anchor(jax.random.fold_in(seeds[7], 71), 0),
        "domain_atoms": draw_domain_atoms(jax.random.fold_in(seeds[7], 71), 0),
        "projector": gaussian(seeds[5], (PROJ, BOX ** 3), (BOX ** 3) ** -0.5, 0.25, (), jnp.float32),
        "strength": jnp.clip(jnp.exp(jax.random.uniform(seeds[6], (PROJ,), jnp.float32, math.log(4.0), math.log(16.0))), 4.0, 16.0),
    }


spacing = 0.5
time_step = 0.05
second_taps = (-205.0 / 72.0, 8.0 / 5.0, -1.0 / 5.0, 8.0 / 315.0, -1.0 / 560.0)
first_taps = (0.0, 4.0 / 5.0, -1.0 / 5.0, 4.0 / 105.0, -1.0 / 280.0)
highest = lax.Precision.HIGHEST


def pad_zeros(field, axis_pos, leading, trailing):
    widths = [(0, 0)] * field.ndim
    widths[axis_pos] = (leading, trailing)
    return jnp.pad(field, widths)


def stencil_sum(padded, axis_pos, length, stencil, symmetric):
    centre = lax.slice_in_dim(padded, 4, 4 + length, axis=axis_pos)
    running = stencil[0] * centre if symmetric else jnp.zeros_like(centre)
    for offset in (1, 2, 3, 4):
        upper_part = lax.slice_in_dim(padded, 4 + offset, 4 + offset + length, axis=axis_pos)
        lower_part = lax.slice_in_dim(padded, 4 - offset, 4 - offset + length, axis=axis_pos)
        if symmetric:
            running = running + stencil[offset] * (upper_part + lower_part)
        else:
            running = running + stencil[offset] * (upper_part - lower_part)
    return running


def box_cells(anchor_rows, shift_x, rows_y, cells_z):
    box_cell = jnp.arange(BOX ** 3).astype(jnp.int32)
    cell_x = box_cell // (BOX * BOX)
    cell_y = (box_cell // BOX) % BOX
    cell_z = box_cell % BOX
    start_x = jnp.maximum(anchor_rows[0] + shift_x, 0)
    plane_pos = start_x[:, None] + cell_x[None, :]
    row_pos = anchor_rows[1][:, None] + cell_y[None, :]
    depth_pos = anchor_rows[2][:, None] + cell_z[None, :]
    return ((plane_pos * rows_y + row_pos) * cells_z + depth_pos).astype(jnp.int32)


def reference(orbitals, potential, laser_field, box_anchor, domain_atoms, projector, strength):
    coord_x = (jnp.arange(NX).astype(jnp.float32) - (NX - 1) / 2.0) * spacing
    coord_y = (jnp.arange(NY).astype(jnp.float32) - (NY - 1) / 2.0) * spacing
    coord_z = (jnp.arange(NZ).astype(jnp.float32) - (NZ - 1) / 2.0) * spacing
    v_total = (potential + laser_field[0] * coord_x[:, None, None]
               + laser_field[1] * coord_y[None, :, None] + laser_field[2] * coord_z[None, None, :])
    listed = domain_atoms.reshape(-1).astype(jnp.int32)
    listed_mask = (listed >= 0).astype(jnp.float32)
    anchor = jnp.take(box_anchor, jnp.maximum(listed, 0), axis=1).astype(jnp.int32)
    owner = (jnp.arange(N_DOM * CAP) // CAP).astype(jnp.int32)
    anchor = anchor.at[0].add(owner * SX)
    cells = box_cells(anchor, 8, NY, NZ).reshape(-1)

    def hamiltonian(field):
        laplace = stencil_sum(pad_zeros(field, 1, 4, 4), 1, NX, second_taps, True)
        laplace = laplace + stencil_sum(pad_zeros(field, 2, 4, 4), 2, NY, second_taps, True)
        laplace = laplace + stencil_sum(pad_zeros(field, 3, 4, 4), 3, NZ, second_taps, True)
        laplace = laplace / (spacing * spacing)
        padded = pad_zeros(field, 1, 8, 8).reshape(2, -1)
        box_values = jnp.take(padded, cells, axis=1).reshape(2, -1, BOX ** 3)
        coeffs = jnp.einsum("csb,pb->csp", box_values, projector, precision=highest) * listed_mask[None, :, None]
        spread = jnp.einsum("csp,pb->csb", coeffs * strength[None, None, :], projector, precision=highest)
        added = jnp.zeros_like(padded).at[:, cells].add(spread.reshape(2, -1))
        projected = added.reshape(2, NX + 16, NY, NZ)[:, 8:NX + 8]
        return -0.5 * laplace + v_total * field + projected

    def one_orbital(carry, orbital_pos):
        density_sum, current_sum = carry
        field = lax.dynamic_index_in_dim(orbitals, orbital_pos, 1, keepdims=False)
        gradients = [stencil_sum(pad_zeros(field, axis_pos, 4, 4), axis_pos, field.shape[axis_pos], first_taps, False) / spacing
                     for axis_pos in (1, 2, 3)]
        flow = jnp.stack([field[0] * gradient[1] - field[1] * gradient[0] for gradient in gradients])
        taylor_term = field
        evolved_pair = field
        for order in range(1, TERMS + 1):
            applied = hamiltonian(taylor_term)
            taylor_term = (time_step / order) * jnp.stack([applied[1], -applied[0]])
            evolved_pair = evolved_pair + taylor_term
        density_sum = density_sum + evolved_pair[0] * evolved_pair[0] + evolved_pair[1] * evolved_pair[1]
        return (density_sum, current_sum + flow), evolved_pair

    start = (jnp.zeros((NX, NY, NZ), jnp.float32), jnp.zeros((3, NX, NY, NZ), jnp.float32))
    (density_sum, current_sum), evolved_all = lax.scan(one_orbital, start, jnp.arange(ORBITALS).astype(jnp.int32))
    scale = 2.0 / ORBITALS
    return jnp.moveaxis(evolved_all, 0, 1), scale * density_sum, scale * current_sum
```

```python
import functools

import jax
import jax.numpy as jnp
from jax import lax
from jax.experimental import pallas as pl
from jax.experimental.pallas import tpu as pltpu
from jax.sharding import PartitionSpec as P

TERMS = 4
BOX = 8
PROJ = 4

spacing = 0.5
time_step = 0.05
second_taps = (-205.0 / 72.0, 8.0 / 5.0, -1.0 / 5.0, 8.0 / 315.0, -1.0 / 560.0)
first_taps = (0.0, 4.0 / 5.0, -1.0 / 5.0, 4.0 / 105.0, -1.0 / 280.0)
kinetic = tuple(-0.5 * tap / (spacing * spacing) for tap in second_taps)
slope = tuple(tap / spacing for tap in first_taps)

VMEM = pl.BlockSpec(memory_space=pltpu.VMEM)
SMEM = pl.BlockSpec(memory_space=pltpu.SMEM)


def shifted(value, offset):
    cells = value.shape[-1]
    lane = lax.broadcasted_iota(jnp.int32, value.shape, value.ndim - 1)
    inside = (lane < cells - offset) if offset > 0 else (lane >= -offset)
    return jnp.where(inside, pltpu.roll(value, (-offset) % cells, value.ndim - 1), 0.0)


def fill_padded(padded, u):
    blocks, rows, cells = u.shape
    padded[:, 0:8, :] = jnp.zeros((blocks, 8, cells), jnp.float32)
    padded[:, 8 + rows : 16 + rows, :] = jnp.zeros((blocks, 8, cells), jnp.float32)
    for b in range(blocks):
        padded[b, 8 : 8 + rows, :] = u[b]


def atom_of(atoms, anchor, row, slot):
    atom = jnp.maximum(atoms[row, slot], 0)
    return anchor[1, atom], anchor[2, atom]


def local_kernel(planes, slots, where, atoms, anchor, u, v, proj, h, partial, padded, sums):
    blocks, rows, cells = u.shape
    fill_padded(padded, u)
    for b in range(blocks):
        plane = b % planes
        centre = u[b]
        total = (v[plane] + 3.0 * kinetic[0]) * centre
        for m in (1, 2, 3, 4):
            near = padded[b, 8 + m : 8 + m + rows, :] + padded[b, 8 - m : 8 - m + rows, :]
            near = near + shifted(centre, m) + shifted(centre, -m)
            if plane + m < planes:
                near = near + u[b + m]
            if plane - m >= 0:
                near = near + u[b - m]
            total = total + kinetic[m] * near
        h[b] = total

    me = where[0]
    behind = jnp.maximum(me - 1, 0)

    def slot_step(slot, carry):
        for side, row in ((0, me), (1, behind)):
            y0, z0 = atom_of(atoms, anchor, row, slot)
            shift = jnp.where(z0 == 0, 0, cells - z0)
            boxes = [pltpu.roll(u[b, pl.ds(y0, BOX), :], shift, 1) for b in range(blocks)]
            lines = []
            for p in range(PROJ):
                for ch in range(2):
                    total = proj[p * BOX + side * planes] * boxes[ch * planes]
                    for i in range(1, planes):
                        total = total + proj[p * BOX + side * planes + i] * boxes[ch * planes + i]
                    lines.append(jnp.sum(total, axis=0, keepdims=True))
            at = pl.multiple_of(side * slots * BOX + slot * BOX, BOX)
            sums[pl.ds(at, BOX), :] = jnp.concatenate(lines, axis=0)
        return carry

    lax.fori_loop(0, slots, slot_step, 0, unroll=2)
    packed = [
        jnp.sum(sums[t * cells : (t + 1) * cells, :].T, axis=0, keepdims=True)
        for t in range(2 * slots * BOX // cells)
    ]
    partial[...] = jnp.concatenate(packed + [jnp.zeros((8 - len(packed), cells), jnp.float32)], axis=0)


def halo_weights(even, taps, mirror):
    pair, other = {}, {}
    for i in range(4):
        for j in range(4):
            above = taps[4 + j - i] if j <= i else 0.0
            below = mirror * taps[4 + i - j] if i <= j else 0.0
            pair[i, j] = jnp.where(even, above, below)
            other[i, j] = jnp.where(even, below, above)
    return pair, other


def finish_kernel(
    planes, slots, factor, last, scale,
    where, atoms, anchor, h, pair_u, other_u, partial, pair_c, other_c, weight, proj, evolved,
    *rest,
):
    if last:
        evolved_out, density, acc, spread = rest
    else:
        u_out, evolved_out, acc, spread = rest
    blocks, rows, cells = h.shape
    me = where[0]
    behind = jnp.maximum(me - 1, 0)
    even = lax.rem(me, 2) == 0
    pair_w, other_w = halo_weights(even, kinetic, 1.0)
    for b in range(blocks):
        plane, first = b % planes, b - b % planes
        total = h[b]
        for j in range(planes):
            total = total + pair_w[plane, j] * pair_u[first + j]
            total = total + other_w[plane, j] * other_u[first + j]
        acc[b] = total

    mine, after, before = partial[...], pair_c[...], other_c[...]
    after, before = jnp.where(even, after, before), jnp.where(even, before, after)
    half = slots * BOX // cells
    for t in range(2 * half):
        got = after[t + half : t + half + 1] if t < half else before[t - half : t - half + 1]
        line = (mine[t : t + 1] + got) * weight[t : t + 1, :]
        spread[t * cells : (t + 1) * cells, :] = jnp.broadcast_to(line, (cells, cells)).T

    def slot_step(slot, carry):
        for side, row in ((0, me), (1, behind)):
            y0, z0 = atom_of(atoms, anchor, row, slot)
            at = pl.multiple_of(side * slots * BOX + slot * BOX, BOX)
            coeffs = spread[pl.ds(at, BOX), :]
            lines = [jnp.broadcast_to(coeffs[q : q + 1], (BOX, cells)) for q in range(2 * PROJ)]
            for ch in range(2):
                for i in range(planes):
                    delta = lines[ch] * proj[side * planes + i]
                    for p in range(1, PROJ):
                        delta = delta + lines[2 * p + ch] * proj[p * BOX + side * planes + i]
                    b = ch * planes + i
                    acc[b, pl.ds(y0, BOX), :] = acc[b, pl.ds(y0, BOX), :] + pltpu.roll(delta, z0, 1)
        return carry

    lax.fori_loop(0, slots, slot_step, 0, unroll=2)
    for plane in range(planes):
        real = factor * acc[planes + plane]
        imag = -factor * acc[plane]
        real_sum = evolved[plane] + real
        imag_sum = evolved[planes + plane] + imag
        evolved_out[plane] = real_sum
        evolved_out[planes + plane] = imag_sum
        if last:
            density[plane] = scale * (real_sum * real_sum + imag_sum * imag_sum)
        else:
            u_out[plane] = real
            u_out[planes + plane] = imag


def current_kernel(planes, scale, where, u, pair_u, other_u, flow, padded):
    blocks, rows, cells = u.shape
    even = lax.rem(where[0], 2) == 0
    pair_w, other_w = halo_weights(even, slope, -1.0)
    fill_padded(padded, u)
    for plane in range(planes):
        gradients = []
        for b in (plane, planes + plane):
            first = b - plane
            along_x = pair_w[plane, 0] * pair_u[first] + other_w[plane, 0] * other_u[first]
            for j in range(1, planes):
                along_x = along_x + pair_w[plane, j] * pair_u[first + j]
                along_x = along_x + other_w[plane, j] * other_u[first + j]
            along_y = along_z = 0.0
            for m in (1, 2, 3, 4):
                if plane + m < planes:
                    along_x = along_x + slope[m] * u[b + m]
                if plane - m >= 0:
                    along_x = along_x - slope[m] * u[b - m]
                along_y = along_y + slope[m] * (
                    padded[b, 8 + m : 8 + m + rows, :] - padded[b, 8 - m : 8 - m + rows, :]
                )
                along_z = along_z + slope[m] * (shifted(u[b], m) - shifted(u[b], -m))
            gradients.append((along_x, along_y, along_z))
        for c in range(3):
            flow[c * planes + plane] = scale * (
                u[plane] * gradients[1][c] - u[planes + plane] * gradients[0][c]
            )


def f32(*shape):
    return jax.ShapeDtypeStruct(shape, jnp.float32)


def body(orbitals, potential, laser_field, box_anchor, domain_atoms, projector, strength):
    planes, rows, cells = orbitals.shape[2:]
    blocks = 2 * planes
    domains = lax.axis_size("dom")
    orbs = lax.axis_size("orb")
    slots = domain_atoms.shape[1]
    me = lax.axis_index("dom")
    where = me.reshape(1).astype(jnp.int32)
    scale = 2.0 / orbs
    params = pltpu.CompilerParams(vmem_limit_bytes=32 * 1024 * 1024)

    pairs = [(i, i ^ 1) for i in range(domains)]
    others = [(i, i + 1) for i in range(1, domains - 1, 2)] + [(i + 1, i) for i in range(1, domains - 1, 2)]

    def exchange(value):
        return lax.ppermute(value, "dom", pairs), lax.ppermute(value, "dom", others)

    u = orbitals.reshape(blocks, rows, cells)
    coord_x = ((me * planes + jnp.arange(planes)).astype(jnp.float32) - (domains * planes - 1) / 2.0) * spacing
    coord_y = (jnp.arange(rows).astype(jnp.float32) - (rows - 1) / 2.0) * spacing
    coord_z = (jnp.arange(cells).astype(jnp.float32) - (cells - 1) / 2.0) * spacing
    v = (
        potential
        + laser_field[0] * coord_x[:, None, None]
        + laser_field[1] * coord_y[None, :, None]
        + laser_field[2] * coord_z[None, None, :]
    )
    proj = jnp.pad(projector.reshape(PROJ * BOX, BOX, BOX), ((0, 0), (0, 0), (0, cells - BOX)))
    own = lax.dynamic_index_in_dim(domain_atoms, me, 0, keepdims=False) >= 0
    behind = lax.dynamic_index_in_dim(domain_atoms, jnp.maximum(me - 1, 0), 0, keepdims=False) >= 0
    listed = jnp.stack([own, behind & (me > 0)]).astype(jnp.float32)
    weight = jnp.broadcast_to(listed[:, :, None, None] * strength[None, None, :, None], (2, slots, PROJ, 2))
    weight = jnp.pad(weight.reshape(-1, cells), ((0, 8 - 2 * slots * BOX // cells), (0, 0)))

    local = pl.pallas_call(
        functools.partial(local_kernel, planes, slots),
        out_shape=(f32(blocks, rows, cells), f32(8, cells)),
        in_specs=[SMEM] * 3 + [VMEM] * 3,
        out_specs=(VMEM, VMEM),
        scratch_shapes=[
            pltpu.VMEM((blocks, rows + 16, cells), jnp.float32),
            pltpu.VMEM((2 * slots * BOX, cells), jnp.float32),
        ],
        compiler_params=params,
        cost_estimate=pl.CostEstimate(flops=8_000_000, bytes_accessed=10_000_000, transcendentals=0),
        name="local_part",
    )

    def finish(order):
        last = order == TERMS
        second = f32(planes, rows, cells) if last else f32(blocks, rows, cells)
        shapes = (f32(blocks, rows, cells), second)
        return pl.pallas_call(
            functools.partial(finish_kernel, planes, slots, time_step / order, last, scale),
            out_shape=shapes if last else (shapes[1], shapes[0]),
            in_specs=[SMEM] * 3 + [VMEM] * 9,
            out_specs=(VMEM, VMEM),
            scratch_shapes=[
                pltpu.VMEM((blocks, rows, cells), jnp.float32),
                pltpu.VMEM((2 * slots * BOX, cells), jnp.float32),
            ],
            compiler_params=params,
            name="finish_part",
        )

    current = pl.pallas_call(
        functools.partial(current_kernel, planes, scale),
        out_shape=f32(3 * planes, rows, cells),
        in_specs=[SMEM] + [VMEM] * 3,
        out_specs=VMEM,
        scratch_shapes=[pltpu.VMEM((blocks, rows + 16, cells), jnp.float32)],
        compiler_params=params,
        cost_estimate=pl.CostEstimate(flops=8_000_000, bytes_accessed=5_000_000, transcendentals=0),
        name="current_part",
    )

    evolved = u
    start = u
    for order in range(1, TERMS + 1):
        pair_u, other_u = exchange(u)
        h, partial = local(where, domain_atoms, box_anchor, u, v, proj)
        pair_c, other_c = exchange(partial)
        if order == 1:
            halos = pair_u, other_u
        first, second = finish(order)(
            where, domain_atoms, box_anchor, h, pair_u, other_u, partial, pair_c, other_c, weight, proj, evolved
        )
        if order < TERMS:
            u, evolved = first, second
        else:
            evolved, density = first, second
        if order == 1:
            flow = current(where, start, *halos)

    fields = jnp.concatenate([density, flow], axis=0)
    fields = jnp.moveaxis(fields, 1, 0)
    fields = lax.all_to_all(fields, "orb", 0, 0, tiled=True)
    fields = jnp.sum(fields, axis=0).reshape(4, planes, 1, cells)
    return evolved.reshape(orbitals.shape), fields[0], fields[1:]


def solution(mesh):
    in_specs = (P(None, "orb", "dom", None, None), P("dom", None, None), P(), P(), P(), P(), P())
    out_specs = (
        P(None, "orb", "dom", None, None),
        P("dom", "orb", None),
        P(None, "dom", "orb", None),
    )
    return jax.shard_map(body, mesh=mesh, in_specs=in_specs, out_specs=out_specs, check_vma=False)
```

```python
import functools

import jax
import jax.numpy as jnp
from jax import lax
from jax.experimental import pallas as pl
from jax.experimental.pallas import tpu as pltpu
from jax.sharding import PartitionSpec as P

TERMS = 4
BOX = 8
PROJ = 4

spacing = 0.5
time_step = 0.05
second_taps = (-205.0 / 72.0, 8.0 / 5.0, -1.0 / 5.0, 8.0 / 315.0, -1.0 / 560.0)
first_taps = (0.0, 4.0 / 5.0, -1.0 / 5.0, 4.0 / 105.0, -1.0 / 280.0)
kinetic = tuple(-0.5 * tap / (spacing * spacing) for tap in second_taps)
slope = tuple(tap / spacing for tap in first_taps)

VMEM = pl.BlockSpec(memory_space=pltpu.VMEM)
SMEM = pl.BlockSpec(memory_space=pltpu.SMEM)


def f32(*shape):
    return jax.ShapeDtypeStruct(shape, jnp.float32)


def shifted(value, offset):
    cells = value.shape[-1]
    lane = lax.broadcasted_iota(jnp.int32, value.shape, value.ndim - 1)
    inside = (lane < cells - offset) if offset > 0 else (lane >= -offset)
    return jnp.where(inside, pltpu.roll(value, (-offset) % cells, value.ndim - 1), 0.0)


def fill_padded(padded, planes, rows, read):
    cells = padded.shape[-1]
    for b in range(planes):
        padded[b, 0:8, :] = jnp.zeros((8, cells), jnp.float32)
        padded[b, 8 + rows : 16 + rows, :] = jnp.zeros((8, cells), jnp.float32)
        padded[b, 8 : 8 + rows, :] = read(b)


def atom_of(atoms, anchor, row, slot):
    atom = jnp.maximum(atoms[row, slot], 0)
    return anchor[1, atom], anchor[2, atom]


def fold(vectors):
    row = lax.broadcasted_iota(jnp.int32, vectors[0].shape, 0)
    for step in (4, 2, 1):
        lower = (row & step) == 0
        merged = []
        for a, b in zip(vectors[:step], vectors[step:]):
            crossed = jnp.where(lower, b, a)
            if step == 4:
                partner = pltpu.roll(crossed, 4, 0)
            else:
                partner = jnp.where(lower, pltpu.roll(crossed, 8 - step, 0), pltpu.roll(crossed, step, 0))
            merged.append(jnp.where(lower, a, b) + partner)
        vectors = merged
    return vectors[0]


def partial_sums(planes, rows, slots, me, atoms, anchor, u, proj, sums):
    cells = u.shape[-1]
    behind = jnp.maximum(me - 1, 0)

    def two_slots(pair, carry):
        for side, row in ((0, me), (1, behind)):
            products = []
            for slot in (2 * pair, 2 * pair + 1):
                y0, z0 = atom_of(atoms, anchor, row, slot)
                shift = jnp.where(z0 == 0, 0, cells - z0)
                boxes = [pltpu.roll(u[pl.ds(i * rows + y0, BOX), :], shift, 1) for i in range(planes)]
                for p in range(PROJ):
                    first = p * BOX + side * planes
                    total = proj[first] * boxes[0]
                    for i in range(1, planes):
                        total = total + proj[first + i] * boxes[i]
                    products.append(total)
            at = pl.multiple_of(side * slots * PROJ + pair * 8, 8)
            sums[pl.ds(at, 8), :] = fold(products)
        return carry

    lax.fori_loop(0, slots // 2, two_slots, 0)
    size = slots * PROJ
    lines = [jnp.sum(sums[side * size : (side + 1) * size, :].T, axis=0, keepdims=True) for side in (0, 1)]
    return jnp.concatenate(lines + [jnp.zeros((6, size), jnp.float32)], axis=0)


def prepare_kernel(
    planes, rows, slots, domains, where, atoms, anchor, laser, strength, potential, projector, u,
    v, proj, weight, partial, sums,
):
    cells = v.shape[-1]
    me = where[0]
    behind = jnp.maximum(me - 1, 0)
    lane = lax.broadcasted_iota(jnp.int32, (8, cells), 1)
    for chunk in range(BOX**3 // cells):
        block = projector[:, chunk * cells : (chunk + 1) * cells]
        for part in range(cells // BOX):
            i, j = chunk * 2 + part // BOX, part % BOX
            moved = block if part == 0 else pltpu.roll(block, cells - part * BOX, 1)
            moved = jnp.where(lane[:PROJ] < BOX, moved, 0.0)
            for p in range(PROJ):
                proj[p * BOX + i, j : j + 1, :] = moved[p : p + 1]

    line = lax.broadcasted_iota(jnp.int32, (8, cells), 0)
    listed = jnp.zeros((8, cells), jnp.float32)
    for slot in range(slots):
        own = jnp.where(atoms[me, slot] >= 0, 1.0, 0.0)
        before = jnp.where((atoms[behind, slot] >= 0) & (me > 0), 1.0, 0.0)
        here = (lane // PROJ) == slot
        listed = jnp.where(here & (line == 0), own, jnp.where(here & (line == 1), before, listed))
    strengths = jnp.zeros((8, cells), jnp.float32)
    for p in range(PROJ):
        strengths = jnp.where((lane % PROJ) == p, strength[p], strengths)
    weight[...] = listed * strengths

    y = lax.broadcasted_iota(jnp.int32, (rows, cells), 0).astype(jnp.float32)
    z = lax.broadcasted_iota(jnp.int32, (rows, cells), 1).astype(jnp.float32)
    along = laser[1] * ((y - (rows - 1) / 2.0) * spacing) + laser[2] * ((z - (cells - 1) / 2.0) * spacing)
    for i in range(planes):
        x = ((me * planes + i).astype(jnp.float32) - (domains * planes - 1) / 2.0) * spacing
        v[i] = potential[i] + laser[0] * x + along + 3.0 * kinetic[0]

    for ch in range(2):
        partial[8 * ch : 8 * ch + 8, :] = partial_sums(
            planes, rows, slots, me, atoms, anchor, u.at[ch], proj, sums
        )


def step_kernel(planes, rows, slots, factor, first, last, scale, *refs):
    refs = list(refs)
    where, atoms, anchor, u, before, after = refs[:6]
    refs = refs[6:]
    size = planes * rows
    if first is not None:
        partials = [ref.at[8 * first : 8 * first + 8] for ref in refs[:3]]
        refs = refs[3:]
    else:
        partials = [ref.at[size : size + 8] for ref in (u, before, after)]
    v, weight, proj, evolved = refs[:4]
    refs = refs[4:]
    if last == "both":
        other, result, density, acc, padded, spread, sums = refs
    elif last:
        result, acc, padded, spread, sums = refs
    else:
        message, result, acc, padded, spread, sums = refs
    cells = v.shape[-1]
    me = where[0]
    behind = jnp.maximum(me - 1, 0)

    def plane_of(ref, i):
        return ref[i * rows : (i + 1) * rows, :]

    fill_padded(padded, planes, rows, lambda i: plane_of(u, i))
    for i in range(planes):
        centre = plane_of(u, i)
        total = v[i] * centre
        for m in (1, 2, 3, 4):
            near = padded[i, 8 + m : 8 + m + rows, :] + padded[i, 8 - m : 8 - m + rows, :]
            near = near + shifted(centre, m) + shifted(centre, -m)
            near = near + (plane_of(u, i + m) if i + m < planes else plane_of(after, i + m - planes))
            near = near + (plane_of(u, i - m) if i >= m else plane_of(before, i - m + planes))
            total = total + kinetic[m] * near
        acc[i * rows : (i + 1) * rows, :] = total

    mine, ahead, back = [ref[...] for ref in partials[:1] + partials[2:] + partials[1:2]]
    for side, got in ((0, ahead[1:2]), (1, back[0:1])):
        line = (mine[side : side + 1] + got) * weight[side : side + 1, :]
        spread[side * cells : (side + 1) * cells, :] = jnp.broadcast_to(line, (cells, cells)).T

    def two_slots(pair, carry):
        for slot in (2 * pair, 2 * pair + 1):
            for side, row in ((0, me), (1, behind)):
                y0, z0 = atom_of(atoms, anchor, row, slot)
                at = side * slots * PROJ + slot * PROJ
                lines = [
                    jnp.broadcast_to(spread[pl.ds(at + p, 1), :], (BOX, cells)) for p in range(PROJ)
                ]
                for i in range(planes):
                    delta = lines[0] * proj[side * planes + i]
                    for p in range(1, PROJ):
                        delta = delta + lines[p] * proj[p * BOX + side * planes + i]
                    at_row = pl.ds(i * rows + y0, BOX)
                    acc[at_row, :] = acc[at_row, :] + pltpu.roll(delta, z0, 1)
        return carry

    lax.fori_loop(0, slots // 2, two_slots, 0)
    for i in range(planes):
        span = slice(i * rows, (i + 1) * rows)
        new = factor * acc[span, :]
        total = evolved[span, :] + new
        if last == "both":
            held = other[span, :]
            result[0, span, :] = held
            result[1, span, :] = total
            density[i] = scale * (held * held + total * total)
        else:
            result[span, :] = total
        if not last:
            message[span, :] = new
    if not last:
        message[size : size + 8, :] = partial_sums(planes, rows, slots, me, atoms, anchor, message, proj, sums)


def current_kernel(planes, rows, scale, u, real_before, real_after, imag_before, imag_after, flow, padded):
    cells = u.shape[-1]
    halos = ((real_before, real_after), (imag_before, imag_after))
    for ch in range(2):
        fill_padded(padded.at[ch], planes, rows, lambda i, ch=ch: u[ch, i * rows : (i + 1) * rows, :])

    def plane_of(ref, i):
        return ref[i * rows : (i + 1) * rows, :]

    for i in range(planes):
        gradients = []
        for ch in range(2):
            own, (before, after) = u.at[ch], halos[ch]
            centre = plane_of(own, i)
            along_x = along_y = along_z = 0.0
            for m in (1, 2, 3, 4):
                upper = plane_of(own, i + m) if i + m < planes else plane_of(after, i + m - planes)
                lower = plane_of(own, i - m) if i >= m else plane_of(before, i - m + planes)
                along_x = along_x + slope[m] * (upper - lower)
                along_y = along_y + slope[m] * (
                    padded[ch, i, 8 + m : 8 + m + rows, :] - padded[ch, i, 8 - m : 8 - m + rows, :]
                )
                along_z = along_z + slope[m] * (shifted(centre, m) - shifted(centre, -m))
            gradients.append((along_x, along_y, along_z))
        for c in range(3):
            flow[c * planes + i] = scale * (
                plane_of(u.at[0], i) * gradients[1][c] - plane_of(u.at[1], i) * gradients[0][c]
            )


def body(orbitals, potential, laser_field, box_anchor, domain_atoms, projector, strength):
    planes, rows, cells = orbitals.shape[2:]
    size = planes * rows
    domains = lax.axis_size("dom")
    orbs = lax.axis_size("orb")
    slots = domain_atoms.shape[1]
    me = lax.axis_index("dom")
    where = me.reshape(1).astype(jnp.int32)
    places = (where, domain_atoms, box_anchor)
    scale = 2.0 / orbs
    params = pltpu.CompilerParams(vmem_limit_bytes=32 * 1024 * 1024)

    up = [(i, i + 1) for i in range(domains - 1)]
    down = [(j, i) for i, j in up]

    def exchange(value):
        return lax.ppermute(value, "dom", up), lax.ppermute(value, "dom", down)

    u = orbitals.reshape(2, size, cells)
    start = [u[0], u[1]]
    halos = [exchange(start[0])]
    sums = pltpu.VMEM((2 * slots * PROJ, cells), jnp.float32)
    v, proj, weight, partial = pl.pallas_call(
        functools.partial(prepare_kernel, planes, rows, slots, domains),
        out_shape=(f32(planes, rows, cells), f32(PROJ * BOX, BOX, cells), f32(8, cells), f32(16, cells)),
        in_specs=[SMEM] * 5 + [VMEM] * 3,
        out_specs=(VMEM,) * 4,
        scratch_shapes=[sums],
        compiler_params=params,
        cost_estimate=pl.CostEstimate(flops=8_000_000, bytes_accessed=10_000_000, transcendentals=0),
        name="prepare_part",
    )(*places, laser_field, strength, potential, projector, u)
    partial_halos = exchange(partial)
    later, partial = lax.optimization_barrier((start[1], partial))
    halos.append(exchange(later))

    def step(order, channel, operands, evolved, other=None):
        factor = time_step / order * (1.0 if (channel + order) % 2 == 0 else -1.0)
        last = False if order < TERMS else ("both" if other is not None else True)
        out = (f32(size, cells),)
        if not last:
            out = (f32(size + 8, cells),) + out
        if last == "both":
            out = (f32(2, size, cells), f32(planes, rows, cells))
        extra = () if other is None else (other,)
        count = len(operands) + 4 + len(extra)
        return pl.pallas_call(
            functools.partial(
                step_kernel, planes, rows, slots, factor, channel if order == 1 else None, last, scale
            ),
            out_shape=out,
            in_specs=[SMEM] * 3 + [VMEM] * count,
            out_specs=(VMEM,) * len(out),
            scratch_shapes=[
                pltpu.VMEM((size, cells), jnp.float32),
                pltpu.VMEM((planes, rows + 16, cells), jnp.float32),
                pltpu.VMEM((2 * slots * PROJ, cells), jnp.float32),
                sums,
            ],
            compiler_params=params,
            cost_estimate=pl.CostEstimate(flops=8_000_000, bytes_accessed=10_000_000, transcendentals=0),
            name="taylor_step",
        )(*places, *operands, v, weight, proj, evolved, *extra)

    totals = [start[0], start[1]]
    held = list(start)
    for order in range(1, TERMS + 1):
        for channel in (0, 1):
            to = (channel + order) % 2
            operands = (held[channel], *halos[channel])
            if order == 1:
                operands += (partial, *partial_halos)
            if order < TERMS:
                held[channel], totals[to] = step(order, channel, operands, totals[to])
            elif channel == 0:
                (totals[to],) = step(order, channel, operands, totals[to])
            else:
                evolved, density = step(order, channel, operands, totals[to], totals[1 - to])
        if order == 1:
            flow = pl.pallas_call(
                functools.partial(current_kernel, planes, rows, scale),
                out_shape=f32(3 * planes, rows, cells),
                in_specs=[VMEM] * 5,
                out_specs=VMEM,
                scratch_shapes=[pltpu.VMEM((2, planes, rows + 16, cells), jnp.float32)],
                compiler_params=params,
                cost_estimate=pl.CostEstimate(flops=8_000_000, bytes_accessed=5_000_000, transcendentals=0),
                name="current_part",
            )(u, *halos[0], *halos[1])
        if order < TERMS:
            halos = [exchange(held[channel]) for channel in (0, 1)]

    fields = jnp.concatenate([density, flow], axis=0)
    fields = jnp.moveaxis(fields, 1, 0)
    fields = lax.all_to_all(fields, "orb", 0, 0, tiled=True)
    fields = jnp.sum(fields, axis=0).reshape(4, planes, 1, cells)
    return evolved.reshape(orbitals.shape), fields[0], fields[1:]


def solution(mesh):
    in_specs = (P(None, "orb", "dom", None, None), P("dom", None, None), P(), P(), P(), P(), P())
    out_specs = (
        P(None, "orb", "dom", None, None),
        P("dom", "orb", None),
        P(None, "dom", "orb", None),
    )
    return jax.shard_map(body, mesh=mesh, in_specs=in_specs, out_specs=out_specs, check_vma=False)
```

```python
import functools

import jax
import jax.numpy as jnp
from jax import lax
from jax.experimental import pallas as pl
from jax.experimental.pallas import tpu as pltpu
from jax.sharding import PartitionSpec as P

TERMS = 4
BOX = 8
PROJ = 4
GROUP = 4

spacing = 0.5
time_step = 0.05
second_taps = (-205.0 / 72.0, 8.0 / 5.0, -1.0 / 5.0, 8.0 / 315.0, -1.0 / 560.0)
first_taps = (0.0, 4.0 / 5.0, -1.0 / 5.0, 4.0 / 105.0, -1.0 / 280.0)
kinetic = tuple(-0.5 * tap / (spacing * spacing) for tap in second_taps)
slope = tuple(tap / spacing for tap in first_taps)

VMEM = pl.BlockSpec(memory_space=pltpu.VMEM)
SMEM = pl.BlockSpec(memory_space=pltpu.SMEM)


def f32(*shape):
    return jax.ShapeDtypeStruct(shape, jnp.float32)


def shifted(value, offset):
    cells = value.shape[-1]
    lane = lax.broadcasted_iota(jnp.int32, value.shape, value.ndim - 1)
    inside = (lane < cells - offset) if offset > 0 else (lane >= -offset)
    return jnp.where(inside, pltpu.roll(value, (-offset) % cells, value.ndim - 1), 0.0)


def fill_padded(padded, planes, rows, read):
    cells = padded.shape[-1]
    for b in range(planes):
        padded[b, 0:8, :] = jnp.zeros((8, cells), jnp.float32)
        padded[b, 8 + rows : 16 + rows, :] = jnp.zeros((8, cells), jnp.float32)
        padded[b, 8 : 8 + rows, :] = read(b)


def atom_of(atoms, anchor, row, slot):
    atom = jnp.maximum(atoms[row, slot], 0)
    return anchor[1, atom], anchor[2, atom]


def fold(vectors):
    row = lax.broadcasted_iota(jnp.int32, vectors[0].shape, 0)
    for step in (4, 2, 1):
        lower = (row & step) == 0
        merged = []
        for a, b in zip(vectors[:step], vectors[step:]):
            crossed = jnp.where(lower, b, a)
            if step == 4:
                partner = pltpu.roll(crossed, 4, 0)
            else:
                partner = jnp.where(lower, pltpu.roll(crossed, 8 - step, 0), pltpu.roll(crossed, step, 0))
            merged.append(jnp.where(lower, a, b) + partner)
        vectors = merged
    return vectors[0]


def partial_sums(planes, rows, slots, me, atoms, anchor, u, proj, sums):
    cells = u.shape[-1]
    behind = jnp.maximum(me - 1, 0)

    def group(index, carry):
        stored = []
        for side, row in ((0, me), (1, behind)):
            for pair in range(GROUP // 2):
                products = []
                for slot in (index * GROUP + 2 * pair, index * GROUP + 2 * pair + 1):
                    y0, z0 = atom_of(atoms, anchor, row, slot)
                    shift = jnp.where(z0 == 0, 0, cells - z0)
                    boxes = [pltpu.roll(u[pl.ds(i * rows + y0, BOX), :], shift, 1) for i in range(planes)]
                    for p in range(PROJ):
                        first = p * BOX + side * planes
                        total = proj[first] * boxes[0]
                        for i in range(1, planes):
                            total = total + proj[first + i] * boxes[i]
                        products.append(total)
                at = side * slots * PROJ + index * GROUP * PROJ + 8 * pair
                stored.append((pl.multiple_of(at, 8), fold(products)))
        for at, value in stored:
            sums[pl.ds(at, 8), :] = value
        return carry

    lax.fori_loop(0, slots // GROUP, group, 0)
    size = slots * PROJ
    lines = [jnp.sum(sums[side * size : (side + 1) * size, :].T, axis=0, keepdims=True) for side in (0, 1)]
    return jnp.concatenate(lines + [jnp.zeros((6, size), jnp.float32)], axis=0)


def halo_weights(even, planes, taps, mirror):
    pair, other = {}, {}
    for i in range(planes):
        for j in range(planes):
            above = taps[planes + j - i] if j <= i else 0.0
            below = mirror * taps[planes + i - j] if i <= j else 0.0
            pair[i, j] = jnp.where(even, above, below)
            other[i, j] = jnp.where(even, below, above)
    return pair, other


def prepare_kernel(
    planes, rows, slots, where, atoms, anchor, strength, projector, u,
    proj, weight, message, sums,
):
    cells = u.shape[-1]
    size = planes * rows
    me = where[0]
    behind = jnp.maximum(me - 1, 0)
    lane = lax.broadcasted_iota(jnp.int32, (8, cells), 1)
    for chunk in range(BOX**3 // cells):
        block = projector[:, chunk * cells : (chunk + 1) * cells]
        for part in range(cells // BOX):
            i, j = chunk * (cells // BOX**2) + part // BOX, part % BOX
            moved = block if part == 0 else pltpu.roll(block, cells - part * BOX, 1)
            moved = jnp.where(lane[:PROJ] < BOX, moved, 0.0)
            for p in range(PROJ):
                proj[p * BOX + i, j : j + 1, :] = moved[p : p + 1]

    line = lax.broadcasted_iota(jnp.int32, (8, cells), 0)
    listed = jnp.zeros((8, cells), jnp.float32)
    for slot in range(slots):
        own = jnp.where(atoms[me, slot] >= 0, 1.0, 0.0)
        before = jnp.where((atoms[behind, slot] >= 0) & (me > 0), 1.0, 0.0)
        here = (lane // PROJ) == slot
        listed = jnp.where(here & (line == 0), own, jnp.where(here & (line == 1), before, listed))
    strengths = jnp.zeros((8, cells), jnp.float32)
    for p in range(PROJ):
        strengths = jnp.where((lane % PROJ) == p, strength[p], strengths)
    weight[...] = listed * strengths

    message[0:size, :] = u[0]
    message[size : size + 8, :] = partial_sums(planes, rows, slots, me, atoms, anchor, u.at[0], proj, sums)


def second_kernel(
    planes, rows, slots, domains, where, atoms, anchor, laser, potential, proj, u, v, message, sums
):
    cells = u.shape[-1]
    size = planes * rows
    me = where[0]
    message[0:size, :] = u[1]
    message[size : size + 8, :] = partial_sums(planes, rows, slots, me, atoms, anchor, u.at[1], proj, sums)
    y = lax.broadcasted_iota(jnp.int32, (rows, cells), 0).astype(jnp.float32)
    z = lax.broadcasted_iota(jnp.int32, (rows, cells), 1).astype(jnp.float32)
    along = laser[1] * ((y - (rows - 1) / 2.0) * spacing) + laser[2] * ((z - (cells - 1) / 2.0) * spacing)
    for i in range(planes):
        x = ((me * planes + i).astype(jnp.float32) - (domains * planes - 1) / 2.0) * spacing
        v[i] = potential[i] + laser[0] * x + along + 3.0 * kinetic[0]


def step_kernel(planes, rows, slots, factor, last, scale, *refs):
    where, atoms, anchor, u, pair_u, other_u, v, weight, proj, evolved, *refs = refs
    size = planes * rows
    if last == "both":
        held, result, density, acc, padded, spread, sums = refs
    elif last:
        result, acc, padded, spread, sums = refs
    else:
        message, result, acc, padded, spread, sums = refs
    cells = v.shape[-1]
    me = where[0]
    behind = jnp.maximum(me - 1, 0)
    even = lax.rem(me, 2) == 0
    pair_w, other_w = halo_weights(even, planes, kinetic, 1.0)

    def plane_of(ref, i):
        return ref[i * rows : (i + 1) * rows, :]

    fill_padded(padded, planes, rows, lambda i: plane_of(u, i))
    for i in range(planes):
        centre = plane_of(u, i)
        total = v[i] * centre
        for m in (1, 2, 3, 4):
            near = padded[i, 8 + m : 8 + m + rows, :] + padded[i, 8 - m : 8 - m + rows, :]
            near = near + shifted(centre, m) + shifted(centre, -m)
            if i + m < planes:
                near = near + plane_of(u, i + m)
            if i >= m:
                near = near + plane_of(u, i - m)
            total = total + kinetic[m] * near
        for j in range(planes):
            total = total + pair_w[i, j] * plane_of(pair_u, j) + other_w[i, j] * plane_of(other_u, j)
        acc[i * rows : (i + 1) * rows, :] = total

    mine, of_pair, of_other = (ref[size : size + 8, :] for ref in (u, pair_u, other_u))
    ahead = jnp.where(even, of_pair, of_other)
    back = jnp.where(even, of_other, of_pair)
    for side, got in ((0, ahead[1:2]), (1, back[0:1])):
        line = (mine[side : side + 1] + got) * weight[side : side + 1, :]
        spread[side * cells : (side + 1) * cells, :] = jnp.broadcast_to(line, (cells, cells)).T

    def group(index, carry):
        added = []
        for slot in [index * GROUP + k for k in range(GROUP)]:
            for side, row in ((0, me), (1, behind)):
                y0, z0 = atom_of(atoms, anchor, row, slot)
                at = side * slots * PROJ + slot * PROJ
                lines = [jnp.broadcast_to(spread[pl.ds(at + p, 1), :], (BOX, cells)) for p in range(PROJ)]
                for i in range(planes):
                    delta = lines[0] * proj[side * planes + i]
                    for p in range(1, PROJ):
                        delta = delta + lines[p] * proj[p * BOX + side * planes + i]
                    added.append((pl.ds(i * rows + y0, BOX), pltpu.roll(delta, z0, 1)))
        for at_rows, delta in added:
            acc[at_rows, :] = acc[at_rows, :] + delta
        return carry

    lax.fori_loop(0, slots // GROUP, group, 0)
    for i in range(planes):
        span = slice(i * rows, (i + 1) * rows)
        new = factor * acc[span, :]
        total = evolved[span, :] + new
        if last == "both":
            real = held[span, :]
            result[0, span, :] = real
            result[1, span, :] = total
            density[i] = scale * (real * real + total * total)
        else:
            result[span, :] = total
        if not last:
            message[span, :] = new
    if not last:
        message[size : size + 8, :] = partial_sums(planes, rows, slots, me, atoms, anchor, message, proj, sums)


def current_kernel(planes, rows, scale, where, u, real_pair, real_other, imag_pair, imag_other, flow, padded):
    halos = ((real_pair, real_other), (imag_pair, imag_other))
    pair_w, other_w = halo_weights(lax.rem(where[0], 2) == 0, planes, slope, -1.0)

    def plane_of(ref, i):
        return ref[i * rows : (i + 1) * rows, :]

    for ch in range(2):
        fill_padded(padded.at[ch], planes, rows, lambda i, ch=ch: plane_of(u.at[ch], i))
    for i in range(planes):
        gradients = []
        for ch in range(2):
            own, (pair, other) = u.at[ch], halos[ch]
            centre = plane_of(own, i)
            along_x = along_y = along_z = 0.0
            for m in (1, 2, 3, 4):
                if i + m < planes:
                    along_x = along_x + slope[m] * plane_of(own, i + m)
                if i >= m:
                    along_x = along_x - slope[m] * plane_of(own, i - m)
                along_y = along_y + slope[m] * (
                    padded[ch, i, 8 + m : 8 + m + rows, :] - padded[ch, i, 8 - m : 8 - m + rows, :]
                )
                along_z = along_z + slope[m] * (shifted(centre, m) - shifted(centre, -m))
            for j in range(planes):
                along_x = along_x + pair_w[i, j] * plane_of(pair, j) + other_w[i, j] * plane_of(other, j)
            gradients.append((along_x, along_y, along_z))
        for c in range(3):
            flow[c * planes + i] = scale * (
                plane_of(u.at[0], i) * gradients[1][c] - plane_of(u.at[1], i) * gradients[0][c]
            )


def gather_kernel(planes, got, density, current):
    total = got[0]
    for source in range(1, got.shape[0]):
        total = total + got[source]
    for i in range(planes):
        density[i] = total[i : i + 1]
        for c in range(3):
            current[c, i] = total[planes * (c + 1) + i : planes * (c + 1) + i + 1]


def body(orbitals, potential, laser_field, box_anchor, domain_atoms, projector, strength):
    planes, rows, cells = orbitals.shape[2:]
    size = planes * rows
    domains = lax.axis_size("dom")
    orbs = lax.axis_size("orb")
    slots = domain_atoms.shape[1]
    me = lax.axis_index("dom")
    where = me.reshape(1).astype(jnp.int32)
    places = (where, domain_atoms, box_anchor)
    scale = 2.0 / orbs

    pairs = [(i, i ^ 1) for i in range(domains)]
    others = [(i, i + 1) for i in range(1, domains - 1, 2)] + [(i + 1, i) for i in range(1, domains - 1, 2)]

    def exchange(value):
        other = lax.ppermute(value, "dom", others)
        return lax.ppermute(value, "dom", pairs), other

    def kernel(function, name, out, scalars, arrays, scratch):
        return pl.pallas_call(
            function,
            out_shape=out,
            in_specs=[SMEM] * scalars + [VMEM] * arrays,
            out_specs=jax.tree.map(lambda _: VMEM, out),
            scratch_shapes=scratch,
            compiler_params=pltpu.CompilerParams(vmem_limit_bytes=32 * 1024 * 1024),
            cost_estimate=pl.CostEstimate(flops=8_000_000, bytes_accessed=10_000_000, transcendentals=0),
            name=name,
        )

    sums = pltpu.VMEM((2 * slots * PROJ, cells), jnp.float32)
    u = orbitals.reshape(2, size, cells)
    proj, weight, first = kernel(
        functools.partial(prepare_kernel, planes, rows, slots),
        "prepare_real",
        (f32(PROJ * BOX, BOX, cells), f32(8, cells), f32(size + 8, cells)),
        4, 2, [sums],
    )(*places, strength, projector, u)
    v, second = kernel(
        functools.partial(second_kernel, planes, rows, slots, domains),
        "prepare_imag",
        (f32(planes, rows, cells), f32(size + 8, cells)),
        4, 3, [sums],
    )(*places, laser_field, potential, proj, u)

    def step(order, channel, halos, evolved, held=None):
        sign = 1.0 if (channel + order) % 2 == 0 else -1.0
        last = False if order < TERMS else ("both" if held is not None else True)
        out = (f32(size, cells),)
        if not last:
            out = (f32(size + 8, cells),) + out
        if last == "both":
            out = (f32(2, size, cells), f32(planes, rows, cells))
        extra = () if held is None else (held,)
        return kernel(
            functools.partial(step_kernel, planes, rows, slots, sign * time_step / order, last, scale),
            "taylor_step", out, 3, 7 + len(extra),
            [
                pltpu.VMEM((size, cells), jnp.float32),
                pltpu.VMEM((planes, rows + 16, cells), jnp.float32),
                pltpu.VMEM((2 * slots * PROJ, cells), jnp.float32),
                sums,
            ],
        )(*places, *halos, v, weight, proj, evolved, *extra)

    terms = [first, second]
    totals = [first, second]
    for order in range(1, TERMS + 1):
        halos = [(term, *exchange(term)) for term in terms]
        for channel in (0, 1):
            to = (channel + order) % 2
            if order < TERMS:
                terms[channel], totals[to] = step(order, channel, halos[channel], totals[to])
            elif channel == 0:
                (totals[to],) = step(order, channel, halos[channel], totals[to])
            else:
                evolved, density = step(order, channel, halos[channel], totals[to], totals[1 - to])
        if order == 1:
            flow = kernel(
                functools.partial(current_kernel, planes, rows, scale),
                "current_part", f32(3 * planes, rows, cells), 1, 5,
                [pltpu.VMEM((2, planes, rows + 16, cells), jnp.float32)],
            )(where, u, *halos[0][1:], *halos[1][1:])

    fields = jnp.concatenate([density, flow], axis=0)
    fields = jnp.moveaxis(fields, 1, 0)
    fields = lax.all_to_all(fields, "orb", 0, 0, tiled=True)
    density, current = kernel(
        functools.partial(gather_kernel, planes),
        "sum_over_orb", (f32(planes, 1, cells), f32(3, planes, 1, cells)), 0, 1, [],
    )(fields)
    return evolved.reshape(orbitals.shape), density, current


def solution(mesh):
    in_specs = (P(None, "orb", "dom", None, None), P("dom", None, None), P(), P(), P(), P(), P())
    out_specs = (
        P(None, "orb", "dom", None, None),
        P("dom", "orb", None),
        P(None, "dom", "orb", None),
    )
    return jax.shard_map(body, mesh=mesh, in_specs=in_specs, out_specs=out_specs, check_vma=False)
```

```python
import functools

import jax
import jax.numpy as jnp
from jax import lax
from jax.experimental import pallas as pl
from jax.experimental.pallas import tpu as pltpu
from jax.sharding import PartitionSpec as P

TERMS = 4
BOX = 8
PROJ = 4
GROUP = 32

spacing = 0.5
time_step = 0.05
second_taps = (-205.0 / 72.0, 8.0 / 5.0, -1.0 / 5.0, 8.0 / 315.0, -1.0 / 560.0)
first_taps = (0.0, 4.0 / 5.0, -1.0 / 5.0, 4.0 / 105.0, -1.0 / 280.0)
kinetic = tuple(-0.5 * tap / (spacing * spacing) for tap in second_taps)
slope = tuple(tap / spacing for tap in first_taps)

VMEM = pl.BlockSpec(memory_space=pltpu.VMEM)
SMEM = pl.BlockSpec(memory_space=pltpu.SMEM)


def f32(*shape):
    return jax.ShapeDtypeStruct(shape, jnp.float32)


def shifted(value, offset):
    cells = value.shape[-1]
    lane = lax.broadcasted_iota(jnp.int32, value.shape, value.ndim - 1)
    inside = (lane < cells - offset) if offset > 0 else (lane >= -offset)
    return jnp.where(inside, pltpu.roll(value, (-offset) % cells, value.ndim - 1), 0.0)


def fill_padded(padded, planes, rows, read):
    cells = padded.shape[-1]
    for b in range(planes):
        padded[b, 0:8, :] = jnp.zeros((8, cells), jnp.float32)
        padded[b, 8 + rows : 16 + rows, :] = jnp.zeros((8, cells), jnp.float32)
        padded[b, 8 : 8 + rows, :] = read(b)


def atom_of(atoms, anchor, row, slot):
    atom = jnp.maximum(atoms[row, slot], 0)
    return anchor[1, atom], anchor[2, atom]


def fold(vectors):
    row = lax.broadcasted_iota(jnp.int32, vectors[0].shape, 0)
    for step in (4, 2, 1):
        lower = (row & step) == 0
        merged = []
        for a, b in zip(vectors[:step], vectors[step:]):
            crossed = jnp.where(lower, b, a)
            if step == 4:
                partner = pltpu.roll(crossed, 4, 0)
            else:
                partner = jnp.where(lower, pltpu.roll(crossed, 8 - step, 0), pltpu.roll(crossed, step, 0))
            merged.append(jnp.where(lower, a, b) + partner)
        vectors = merged
    return vectors[0]


def partial_sums(planes, rows, slots, me, atoms, anchor, u, proj, sums):
    cells = u.shape[-1]
    behind = jnp.maximum(me - 1, 0)

    def group(index, carry):
        stored = []
        for side, row in ((0, me), (1, behind)):
            for pair in range(GROUP // 2):
                products = []
                for slot in (index * GROUP + 2 * pair, index * GROUP + 2 * pair + 1):
                    y0, z0 = atom_of(atoms, anchor, row, slot)
                    shift = jnp.where(z0 == 0, 0, cells - z0)
                    boxes = [pltpu.roll(u[pl.ds(i * rows + y0, BOX), :], shift, 1) for i in range(planes)]
                    for p in range(PROJ):
                        first = p * BOX + side * planes
                        total = proj[first] * boxes[0]
                        for i in range(1, planes):
                            total = total + proj[first + i] * boxes[i]
                        products.append(total)
                at = side * slots * PROJ + index * GROUP * PROJ + 8 * pair
                stored.append((pl.multiple_of(at, 8), fold(products)))
        for at, value in stored:
            sums[pl.ds(at, 8), :] = value
        return carry

    lax.fori_loop(0, slots // GROUP, group, 0)
    size = slots * PROJ
    lines = [jnp.sum(sums[side * size : (side + 1) * size, :].T, axis=0, keepdims=True) for side in (0, 1)]
    return jnp.concatenate(lines + [jnp.zeros((6, size), jnp.float32)], axis=0)


def halo_weights(even, planes, taps, mirror):
    pair, other = {}, {}
    for i in range(planes):
        for j in range(planes):
            above = taps[planes + j - i] if j <= i else 0.0
            below = mirror * taps[planes + i - j] if i <= j else 0.0
            pair[i, j] = jnp.where(even, above, below)
            other[i, j] = jnp.where(even, below, above)
    return pair, other


def prepare_kernel(
    planes, rows, slots, where, atoms, anchor, strength, projector, u,
    proj, weight, message, sums,
):
    cells = u.shape[-1]
    size = planes * rows
    me = where[0]
    behind = jnp.maximum(me - 1, 0)
    lane = lax.broadcasted_iota(jnp.int32, (8, cells), 1)
    for chunk in range(BOX**3 // cells):
        block = projector[:, chunk * cells : (chunk + 1) * cells]
        for part in range(cells // BOX):
            i, j = chunk * (cells // BOX**2) + part // BOX, part % BOX
            moved = block if part == 0 else pltpu.roll(block, cells - part * BOX, 1)
            moved = jnp.where(lane[:PROJ] < BOX, moved, 0.0)
            for p in range(PROJ):
                proj[p * BOX + i, j : j + 1, :] = moved[p : p + 1]

    line = lax.broadcasted_iota(jnp.int32, (8, cells), 0)
    listed = jnp.zeros((8, cells), jnp.float32)
    for slot in range(slots):
        own = jnp.where(atoms[me, slot] >= 0, 1.0, 0.0)
        before = jnp.where((atoms[behind, slot] >= 0) & (me > 0), 1.0, 0.0)
        here = (lane // PROJ) == slot
        listed = jnp.where(here & (line == 0), own, jnp.where(here & (line == 1), before, listed))
    strengths = jnp.zeros((8, cells), jnp.float32)
    for p in range(PROJ):
        strengths = jnp.where((lane % PROJ) == p, strength[p], strengths)
    weight[...] = listed * strengths

    message[0:size, :] = u[0]
    message[size : size + 8, :] = partial_sums(planes, rows, slots, me, atoms, anchor, u.at[0], proj, sums)


def second_kernel(
    planes, rows, slots, domains, where, atoms, anchor, laser, potential, proj, u, v, message, sums
):
    cells = u.shape[-1]
    size = planes * rows
    me = where[0]
    message[0:size, :] = u[1]
    message[size : size + 8, :] = partial_sums(planes, rows, slots, me, atoms, anchor, u.at[1], proj, sums)
    y = lax.broadcasted_iota(jnp.int32, (rows, cells), 0).astype(jnp.float32)
    z = lax.broadcasted_iota(jnp.int32, (rows, cells), 1).astype(jnp.float32)
    along = laser[1] * ((y - (rows - 1) / 2.0) * spacing) + laser[2] * ((z - (cells - 1) / 2.0) * spacing)
    for i in range(planes):
        x = ((me * planes + i).astype(jnp.float32) - (domains * planes - 1) / 2.0) * spacing
        v[i] = potential[i] + laser[0] * x + along + 3.0 * kinetic[0]


def step_kernel(planes, rows, slots, factor, last, scale, *refs):
    where, atoms, anchor, u, pair_u, other_u, v, weight, proj, evolved, *refs = refs
    size = planes * rows
    if last == "both":
        held, result, density, acc, padded, spread, sums = refs
    elif last:
        result, acc, padded, spread, sums = refs
    else:
        message, result, acc, padded, spread, sums = refs
    cells = v.shape[-1]
    me = where[0]
    behind = jnp.maximum(me - 1, 0)
    even = lax.rem(me, 2) == 0
    pair_w, other_w = halo_weights(even, planes, kinetic, 1.0)

    def plane_of(ref, i):
        return ref[i * rows : (i + 1) * rows, :]

    fill_padded(padded, planes, rows, lambda i: plane_of(u, i))
    for i in range(planes):
        centre = plane_of(u, i)
        total = v[i] * centre
        for m in (1, 2, 3, 4):
            near = padded[i, 8 + m : 8 + m + rows, :] + padded[i, 8 - m : 8 - m + rows, :]
            near = near + shifted(centre, m) + shifted(centre, -m)
            if i + m < planes:
                near = near + plane_of(u, i + m)
            if i >= m:
                near = near + plane_of(u, i - m)
            total = total + kinetic[m] * near
        for j in range(planes):
            total = total + pair_w[i, j] * plane_of(pair_u, j) + other_w[i, j] * plane_of(other_u, j)
        acc[i * rows : (i + 1) * rows, :] = total

    mine, of_pair, of_other = (ref[size : size + 8, :] for ref in (u, pair_u, other_u))
    ahead = jnp.where(even, of_pair, of_other)
    back = jnp.where(even, of_other, of_pair)
    for side, got in ((0, ahead[1:2]), (1, back[0:1])):
        line = (mine[side : side + 1] + got) * weight[side : side + 1, :]
        spread[side * cells : (side + 1) * cells, :] = jnp.broadcast_to(line, (cells, cells)).T

    def group(index, carry):
        added = []
        for slot in [index * GROUP + k for k in range(GROUP)]:
            for side, row in ((0, me), (1, behind)):
                y0, z0 = atom_of(atoms, anchor, row, slot)
                at = side * slots * PROJ + slot * PROJ
                lines = [jnp.broadcast_to(spread[pl.ds(at + p, 1), :], (BOX, cells)) for p in range(PROJ)]
                for i in range(planes):
                    delta = lines[0] * proj[side * planes + i]
                    for p in range(1, PROJ):
                        delta = delta + lines[p] * proj[p * BOX + side * planes + i]
                    added.append((pl.ds(i * rows + y0, BOX), pltpu.roll(delta, z0, 1)))
        for at_rows, delta in added:
            acc[at_rows, :] = acc[at_rows, :] + delta
        return carry

    lax.fori_loop(0, slots // GROUP, group, 0)
    for i in range(planes):
        span = slice(i * rows, (i + 1) * rows)
        new = factor * acc[span, :]
        total = evolved[span, :] + new
        if last == "both":
            real = held[span, :]
            result[0, span, :] = real
            result[1, span, :] = total
            density[i] = scale * (real * real + total * total)
        else:
            result[span, :] = total
        if not last:
            message[span, :] = new
    if not last:
        message[size : size + 8, :] = partial_sums(planes, rows, slots, me, atoms, anchor, message, proj, sums)


def current_kernel(planes, rows, scale, where, u, real_pair, real_other, imag_pair, imag_other, flow, padded):
    halos = ((real_pair, real_other), (imag_pair, imag_other))
    pair_w, other_w = halo_weights(lax.rem(where[0], 2) == 0, planes, slope, -1.0)

    def plane_of(ref, i):
        return ref[i * rows : (i + 1) * rows, :]

    for ch in range(2):
        fill_padded(padded.at[ch], planes, rows, lambda i, ch=ch: plane_of(u.at[ch], i))
    for i in range(planes):
        gradients = []
        for ch in range(2):
            own, (pair, other) = u.at[ch], halos[ch]
            centre = plane_of(own, i)
            along_x = along_y = along_z = 0.0
            for m in (1, 2, 3, 4):
                if i + m < planes:
                    along_x = along_x + slope[m] * plane_of(own, i + m)
                if i >= m:
                    along_x = along_x - slope[m] * plane_of(own, i - m)
                along_y = along_y + slope[m] * (
                    padded[ch, i, 8 + m : 8 + m + rows, :] - padded[ch, i, 8 - m : 8 - m + rows, :]
                )
                along_z = along_z + slope[m] * (shifted(centre, m) - shifted(centre, -m))
            for j in range(planes):
                along_x = along_x + pair_w[i, j] * plane_of(pair, j) + other_w[i, j] * plane_of(other, j)
            gradients.append((along_x, along_y, along_z))
        for c in range(3):
            flow[c * planes + i] = scale * (
                plane_of(u.at[0], i) * gradients[1][c] - plane_of(u.at[1], i) * gradients[0][c]
            )


def gather_kernel(planes, got, density, current):
    total = got[0]
    for source in range(1, got.shape[0]):
        total = total + got[source]
    for i in range(planes):
        density[i] = total[i : i + 1]
        for c in range(3):
            current[c, i] = total[planes * (c + 1) + i : planes * (c + 1) + i + 1]


def body(orbitals, potential, laser_field, box_anchor, domain_atoms, projector, strength):
    planes, rows, cells = orbitals.shape[2:]
    size = planes * rows
    domains = lax.axis_size("dom")
    orbs = lax.axis_size("orb")
    slots = domain_atoms.shape[1]
    me = lax.axis_index("dom")
    where = me.reshape(1).astype(jnp.int32)
    places = (where, domain_atoms, box_anchor)
    scale = 2.0 / orbs

    pairs = [(i, i ^ 1) for i in range(domains)]
    others = [(i, i + 1) for i in range(1, domains - 1, 2)] + [(i + 1, i) for i in range(1, domains - 1, 2)]

    def exchange(value):
        other = lax.ppermute(value, "dom", others)
        return lax.ppermute(value, "dom", pairs), other

    def kernel(function, name, out, scalars, arrays, scratch):
        return pl.pallas_call(
            function,
            out_shape=out,
            in_specs=[SMEM] * scalars + [VMEM] * arrays,
            out_specs=jax.tree.map(lambda _: VMEM, out),
            scratch_shapes=scratch,
            compiler_params=pltpu.CompilerParams(vmem_limit_bytes=32 * 1024 * 1024),
            cost_estimate=pl.CostEstimate(flops=8_000_000, bytes_accessed=10_000_000, transcendentals=0),
            name=name,
        )

    sums = pltpu.VMEM((2 * slots * PROJ, cells), jnp.float32)
    u = orbitals.reshape(2, size, cells)
    proj, weight, first = kernel(
        functools.partial(prepare_kernel, planes, rows, slots),
        "prepare_real",
        (f32(PROJ * BOX, BOX, cells), f32(8, cells), f32(size + 8, cells)),
        4, 2, [sums],
    )(*places, strength, projector, u)
    v, second = kernel(
        functools.partial(second_kernel, planes, rows, slots, domains),
        "prepare_imag",
        (f32(planes, rows, cells), f32(size + 8, cells)),
        4, 3, [sums],
    )(*places, laser_field, potential, proj, u)

    def step(order, channel, halos, evolved, held=None):
        sign = 1.0 if (channel + order) % 2 == 0 else -1.0
        last = False if order < TERMS else ("both" if held is not None else True)
        out = (f32(size, cells),)
        if not last:
            out = (f32(size + 8, cells),) + out
        if last == "both":
            out = (f32(2, size, cells), f32(planes, rows, cells))
        extra = () if held is None else (held,)
        return kernel(
            functools.partial(step_kernel, planes, rows, slots, sign * time_step / order, last, scale),
            "taylor_step", out, 3, 7 + len(extra),
            [
                pltpu.VMEM((size, cells), jnp.float32),
                pltpu.VMEM((planes, rows + 16, cells), jnp.float32),
                pltpu.VMEM((2 * slots * PROJ, cells), jnp.float32),
                sums,
            ],
        )(*places, *halos, v, weight, proj, evolved, *extra)

    terms = [first, second]
    totals = [first, second]
    for order in range(1, TERMS + 1):
        halos = [(term, *exchange(term)) for term in terms]
        for channel in (0, 1):
            to = (channel + order) % 2
            if order < TERMS:
                terms[channel], totals[to] = step(order, channel, halos[channel], totals[to])
            elif channel == 0:
                (totals[to],) = step(order, channel, halos[channel], totals[to])
            else:
                evolved, density = step(order, channel, halos[channel], totals[to], totals[1 - to])
        if order == 1:
            flow = kernel(
                functools.partial(current_kernel, planes, rows, scale),
                "current_part", f32(3 * planes, rows, cells), 1, 5,
                [pltpu.VMEM((2, planes, rows + 16, cells), jnp.float32)],
            )(where, u, *halos[0][1:], *halos[1][1:])

    fields = jnp.concatenate([density, flow], axis=0)
    fields = jnp.moveaxis(fields, 1, 0)
    fields = lax.all_to_all(fields, "orb", 0, 0, tiled=True)
    density, current = kernel(
        functools.partial(gather_kernel, planes),
        "sum_over_orb", (f32(planes, 1, cells), f32(3, planes, 1, cells)), 0, 1, [],
    )(fields)
    return evolved.reshape(orbitals.shape), density, current


def solution(mesh):
    in_specs = (P(None, "orb", "dom", None, None), P("dom", None, None), P(), P(), P(), P(), P())
    out_specs = (
        P(None, "orb", "dom", None, None),
        P("dom", "orb", None),
        P(None, "dom", "orb", None),
    )
    return jax.shard_map(body, mesh=mesh, in_specs=in_specs, out_specs=out_specs, check_vma=False)
```

```python
import functools

import jax
import jax.numpy as jnp
from jax import lax
from jax.experimental import pallas as pl
from jax.experimental.pallas import tpu as pltpu
from jax.sharding import PartitionSpec as P

TERMS = 4
BOX = 8
PROJ = 4
GROUP = 32
RUN = 3

spacing = 0.5
time_step = 0.05
second_taps = (-205.0 / 72.0, 8.0 / 5.0, -1.0 / 5.0, 8.0 / 315.0, -1.0 / 560.0)
first_taps = (0.0, 4.0 / 5.0, -1.0 / 5.0, 4.0 / 105.0, -1.0 / 280.0)
kinetic = tuple(-0.5 * tap / (spacing * spacing) for tap in second_taps)
slope = tuple(tap / spacing for tap in first_taps)

VMEM = pl.BlockSpec(memory_space=pltpu.VMEM)
SMEM = pl.BlockSpec(memory_space=pltpu.SMEM)
ANY = pl.BlockSpec(memory_space=pl.ANY)


def f32(*shape):
    return jax.ShapeDtypeStruct(shape, jnp.float32)


def shifted(value, offset):
    cells = value.shape[-1]
    lane = lax.broadcasted_iota(jnp.int32, value.shape, value.ndim - 1)
    inside = (lane < cells - offset) if offset > 0 else (lane >= -offset)
    return jnp.where(inside, pltpu.roll(value, (-offset) % cells, value.ndim - 1), 0.0)


def fill_padded(padded, planes, rows, read):
    cells = padded.shape[-1]
    for b in range(planes):
        padded[b, 0:8, :] = jnp.zeros((8, cells), jnp.float32)
        padded[b, 8 + rows : 16 + rows, :] = jnp.zeros((8, cells), jnp.float32)
        padded[b, 8 : 8 + rows, :] = read(b)


def atom_of(atoms, anchor, row, slot):
    atom = jnp.maximum(atoms[row, slot], 0)
    return anchor[1, atom], anchor[2, atom]


def fold(vectors):
    row = lax.broadcasted_iota(jnp.int32, vectors[0].shape, 0)
    for step in (4, 2, 1):
        lower = (row & step) == 0
        merged = []
        for a, b in zip(vectors[:step], vectors[step:]):
            crossed = jnp.where(lower, b, a)
            if step == 4:
                partner = pltpu.roll(crossed, 4, 0)
            else:
                partner = jnp.where(lower, pltpu.roll(crossed, 8 - step, 0), pltpu.roll(crossed, step, 0))
            merged.append(jnp.where(lower, a, b) + partner)
        vectors = merged
    return vectors[0]


def partial_sums(planes, rows, slots, me, atoms, anchor, u, proj, sums):
    cells = u.shape[-1]
    behind = jnp.maximum(me - 1, 0)

    def group(index, carry):
        stored = []
        for side, row in ((0, me), (1, behind)):
            for pair in range(GROUP // 2):
                products = []
                for slot in (index * GROUP + 2 * pair, index * GROUP + 2 * pair + 1):
                    y0, z0 = atom_of(atoms, anchor, row, slot)
                    shift = jnp.where(z0 == 0, 0, cells - z0)
                    boxes = [pltpu.roll(u[pl.ds(i * rows + y0, BOX), :], shift, 1) for i in range(planes)]
                    for p in range(PROJ):
                        first = p * BOX + side * planes
                        total = proj[first] * boxes[0]
                        for i in range(1, planes):
                            total = total + proj[first + i] * boxes[i]
                        products.append(total)
                at = side * slots * PROJ + index * GROUP * PROJ + 8 * pair
                stored.append((pl.multiple_of(at, 8), fold(products)))
        for at, value in stored:
            sums[pl.ds(at, 8), :] = value
        return carry

    lax.fori_loop(0, slots // GROUP, group, 0)
    size = slots * PROJ
    lines = [jnp.sum(sums[side * size : (side + 1) * size, :].T, axis=0, keepdims=True) for side in (0, 1)]
    return jnp.concatenate(lines + [jnp.zeros((6, size), jnp.float32)], axis=0)


def halo_weights(even, planes, taps, mirror):
    pair, other = {}, {}
    for i in range(planes):
        for j in range(planes):
            above = taps[planes + j - i] if j <= i else 0.0
            below = mirror * taps[planes + i - j] if i <= j else 0.0
            pair[i, j] = jnp.where(even, above, below)
            other[i, j] = jnp.where(even, below, above)
    return pair, other


def prepare_kernel(
    planes, rows, slots, where, atoms, anchor, strength, projector_far, u,
    proj, weight, message, sums, projector, sems,
):
    cells = u.shape[-1]
    size = planes * rows
    fetch = pltpu.make_async_copy(u.at[0], message.at[0:size], sems.at[0])
    fetch_projector = pltpu.make_async_copy(projector_far, projector, sems.at[1])
    fetch.start()
    fetch_projector.start()
    me = where[0]
    behind = jnp.maximum(me - 1, 0)
    lane = lax.broadcasted_iota(jnp.int32, (8, cells), 1)
    line = lax.broadcasted_iota(jnp.int32, (8, cells), 0)
    listed = jnp.zeros((8, cells), jnp.float32)
    for slot in range(slots):
        own = jnp.where(atoms[me, slot] >= 0, 1.0, 0.0)
        before = jnp.where((atoms[behind, slot] >= 0) & (me > 0), 1.0, 0.0)
        here = (lane // PROJ) == slot
        listed = jnp.where(here & (line == 0), own, jnp.where(here & (line == 1), before, listed))
    strengths = jnp.zeros((8, cells), jnp.float32)
    for p in range(PROJ):
        strengths = jnp.where((lane % PROJ) == p, strength[p], strengths)
    weight[...] = listed * strengths

    fetch_projector.wait()
    for chunk in range(BOX**3 // cells):
        block = projector[:, chunk * cells : (chunk + 1) * cells]
        for part in range(cells // BOX):
            i, j = chunk * (cells // BOX**2) + part // BOX, part % BOX
            moved = block if part == 0 else pltpu.roll(block, cells - part * BOX, 1)
            moved = jnp.where(lane[:PROJ] < BOX, moved, 0.0)
            for p in range(PROJ):
                proj[p * BOX + i, j : j + 1, :] = moved[p : p + 1]

    fetch.wait()
    message[size : size + 8, :] = partial_sums(planes, rows, slots, me, atoms, anchor, message, proj, sums)


def second_kernel(
    planes, rows, slots, domains, where, atoms, anchor, laser, potential, proj, u, v, message, sums, sem
):
    cells = u.shape[-1]
    size = planes * rows
    me = where[0]
    fetch = pltpu.make_async_copy(u.at[1], message.at[0:size], sem)
    fetch.start()
    y = lax.broadcasted_iota(jnp.int32, (rows, cells), 0).astype(jnp.float32)
    z = lax.broadcasted_iota(jnp.int32, (rows, cells), 1).astype(jnp.float32)
    along = laser[1] * ((y - (rows - 1) / 2.0) * spacing) + laser[2] * ((z - (cells - 1) / 2.0) * spacing)
    for i in range(planes):
        x = ((me * planes + i).astype(jnp.float32) - (domains * planes - 1) / 2.0) * spacing
        v[i] = potential[i] + laser[0] * x + along + 3.0 * kinetic[0]
    fetch.wait()
    message[size : size + 8, :] = partial_sums(planes, rows, slots, me, atoms, anchor, message, proj, sums)


def step_kernel(planes, rows, slots, factor, last, scale, *refs):
    where, atoms, anchor, u, pair_u, other_u, v, weight, proj, evolved, *refs = refs
    size = planes * rows
    if last == "both":
        held, result, density, acc, padded, spread, sums = refs
    elif last:
        result, acc, padded, spread, sums = refs
    else:
        message, result, acc, padded, spread, sums = refs
    cells = v.shape[-1]
    me = where[0]
    behind = jnp.maximum(me - 1, 0)
    even = lax.rem(me, 2) == 0
    pair_w, other_w = halo_weights(even, planes, kinetic, 1.0)

    def plane_of(ref, i):
        return ref[i * rows : (i + 1) * rows, :]

    fill_padded(padded, planes, rows, lambda i: plane_of(u, i))
    for i in range(planes):
        centre = plane_of(u, i)
        total = v[i] * centre
        for m in (1, 2, 3, 4):
            near = padded[i, 8 + m : 8 + m + rows, :] + padded[i, 8 - m : 8 - m + rows, :]
            near = near + shifted(centre, m) + shifted(centre, -m)
            if i + m < planes:
                near = near + plane_of(u, i + m)
            if i >= m:
                near = near + plane_of(u, i - m)
            total = total + kinetic[m] * near
        for j in range(planes):
            total = total + pair_w[i, j] * plane_of(pair_u, j) + other_w[i, j] * plane_of(other_u, j)
        acc[i * rows : (i + 1) * rows, :] = total

    mine, of_pair, of_other = (ref[size : size + 8, :] for ref in (u, pair_u, other_u))
    ahead = jnp.where(even, of_pair, of_other)
    back = jnp.where(even, of_other, of_pair)
    for side, got in ((0, ahead[1:2]), (1, back[0:1])):
        line = (mine[side : side + 1] + got) * weight[side : side + 1, :]
        spread[side * cells : (side + 1) * cells, :] = jnp.broadcast_to(line, (cells, cells)).T

    def group(index, carry):
        added = []
        for slot in [index * GROUP + k for k in range(GROUP)]:
            for side, row in ((0, me), (1, behind)):
                y0, z0 = atom_of(atoms, anchor, row, slot)
                at = side * slots * PROJ + slot * PROJ
                lines = [jnp.broadcast_to(spread[pl.ds(at + p, 1), :], (BOX, cells)) for p in range(PROJ)]
                for i in range(planes):
                    delta = lines[0] * proj[side * planes + i]
                    for p in range(1, PROJ):
                        delta = delta + lines[p] * proj[p * BOX + side * planes + i]
                    added.append((pl.ds(i * rows + y0, BOX), pltpu.roll(delta, z0, 1)))
        for at_rows, delta in added:
            acc[at_rows, :] = acc[at_rows, :] + delta
        return carry

    lax.fori_loop(0, slots // GROUP, group, 0)
    for i in range(planes):
        span = slice(i * rows, (i + 1) * rows)
        new = factor * acc[span, :]
        total = evolved[span, :] + new
        if last == "both":
            real = held[span, :]
            result[0, span, :] = real
            result[1, span, :] = total
            density[i] = scale * (real * real + total * total)
        else:
            result[span, :] = total
        if not last:
            message[span, :] = new
    if not last:
        message[size : size + 8, :] = partial_sums(planes, rows, slots, me, atoms, anchor, message, proj, sums)


def current_kernel(
    planes, rows, scale, where, spot, real, imag, real_pair, real_other, imag_pair, imag_other, keep, send, padded
):
    halos = ((real, real_pair, real_other), (imag, imag_pair, imag_other))
    pair_w, other_w = halo_weights(lax.rem(where[0], 2) == 0, planes, slope, -1.0)
    lower = lax.rem(spot[0], 2) == 0

    def plane_of(ref, i):
        return ref[i * rows : (i + 1) * rows, :]

    for ch in range(2):
        fill_padded(padded.at[ch], planes, rows, lambda i, ch=ch: plane_of(halos[ch][0], i))
    flows = {}
    for i in range(planes):
        gradients = []
        for ch in range(2):
            own, pair, other = halos[ch]
            centre = plane_of(own, i)
            along_x = along_y = along_z = 0.0
            for m in (1, 2, 3, 4):
                if i + m < planes:
                    along_x = along_x + slope[m] * plane_of(own, i + m)
                if i >= m:
                    along_x = along_x - slope[m] * plane_of(own, i - m)
                along_y = along_y + slope[m] * (
                    padded[ch, i, 8 + m : 8 + m + rows, :] - padded[ch, i, 8 - m : 8 - m + rows, :]
                )
                along_z = along_z + slope[m] * (shifted(centre, m) - shifted(centre, -m))
            for j in range(planes):
                along_x = along_x + pair_w[i, j] * plane_of(pair, j) + other_w[i, j] * plane_of(other, j)
            gradients.append((along_x, along_y, along_z))
        half = planes // 2
        for c in range(3):
            flow = scale * (plane_of(real, i) * gradients[1][c] - plane_of(imag, i) * gradients[0][c])
            at = c * half + i % half
            if i < half:
                keep[at] = flow
            else:
                first = keep[at]
                keep[at] = jnp.where(lower, first, flow)
                send[at] = jnp.where(lower, flow, first)


def merge_kernel(spot, held, got, keep, send):
    lower = lax.rem(spot[0] // 2, 2) == 0
    for c in range(3):
        first = held[2 * c] + got[2 * c]
        second = held[2 * c + 1] + got[2 * c + 1]
        keep[c] = jnp.where(lower, first, second)
        send[c] = jnp.where(lower, second, first)


def plane_kept(source):
    x = source // RUN
    return 2 * (x % 2) + x // 2 % 2


def gather_kernel(planes, got, density, current):
    totals = [None] * planes
    for source in range(got.shape[0]):
        p = plane_kept(source)
        totals[p] = got[source] if totals[p] is None else totals[p] + got[source]
    everywhere = totals[0] + totals[1] + totals[2] + totals[3]
    for i in range(planes):
        density[i] = everywhere[i : i + 1]
        for c in range(3):
            current[c, i] = totals[i][planes + c : planes + c + 1]


def body(orbitals, potential, laser_field, box_anchor, domain_atoms, projector, strength):
    planes, rows, cells = orbitals.shape[2:]
    size = planes * rows
    domains = lax.axis_size("dom")
    orbs = lax.axis_size("orb")
    slots = domain_atoms.shape[1]
    me = lax.axis_index("dom")
    where = me.reshape(1).astype(jnp.int32)
    places = (where, domain_atoms, box_anchor)
    spot = (lax.axis_index("orb") // RUN).reshape(1).astype(jnp.int32)
    scale = 2.0 / orbs

    pairs = [(i, i ^ 1) for i in range(domains)]
    others = [(i, i + 1) for i in range(1, domains - 1, 2)] + [(i + 1, i) for i in range(1, domains - 1, 2)]

    def exchange(value):
        other = lax.ppermute(value, "dom", others)
        return lax.ppermute(value, "dom", pairs), other

    def kernel(function, name, out, scalars, arrays, scratch, far=0):
        return pl.pallas_call(
            function,
            out_shape=out,
            in_specs=[SMEM] * scalars + [VMEM] * arrays + [ANY] * far,
            out_specs=jax.tree.map(lambda _: VMEM, out),
            scratch_shapes=scratch,
            compiler_params=pltpu.CompilerParams(vmem_limit_bytes=32 * 1024 * 1024),
            cost_estimate=pl.CostEstimate(flops=8_000_000, bytes_accessed=10_000_000, transcendentals=0),
            name=name,
        )

    sums = pltpu.VMEM((2 * slots * PROJ, cells), jnp.float32)
    u = orbitals.reshape(2, size, cells)
    proj, weight, first = kernel(
        functools.partial(prepare_kernel, planes, rows, slots),
        "prepare_real",
        (f32(PROJ * BOX, BOX, cells), f32(8, cells), f32(size + 8, cells)),
        4, 0,
        [sums, pltpu.VMEM((PROJ, BOX**3), jnp.float32), pltpu.SemaphoreType.DMA((2,))],
        2,
    )(*places, strength, projector, u)
    v, second = kernel(
        functools.partial(second_kernel, planes, rows, slots, domains),
        "prepare_imag",
        (f32(planes, rows, cells), f32(size + 8, cells)),
        4, 2, [sums, pltpu.SemaphoreType.DMA], 1,
    )(*places, laser_field, potential, proj, u)

    def step(order, channel, halos, evolved, held=None):
        sign = 1.0 if (channel + order) % 2 == 0 else -1.0
        last = False if order < TERMS else ("both" if held is not None else True)
        out = (f32(size, cells),)
        if not last:
            out = (f32(size + 8, cells),) + out
        if last == "both":
            out = (f32(2, size, cells), f32(planes, rows, cells))
        extra = () if held is None else (held,)
        return kernel(
            functools.partial(step_kernel, planes, rows, slots, sign * time_step / order, last, scale),
            "taylor_step", out, 3, 7 + len(extra),
            [
                pltpu.VMEM((size, cells), jnp.float32),
                pltpu.VMEM((planes, rows + 16, cells), jnp.float32),
                pltpu.VMEM((2 * slots * PROJ, cells), jnp.float32),
                sums,
            ],
        )(*places, *halos, v, weight, proj, evolved, *extra)

    terms = [first, second]
    totals = [first, second]
    for order in range(1, TERMS + 1):
        halos = [(term, *exchange(term)) for term in terms]
        for channel in (0, 1):
            to = (channel + order) % 2
            if order < TERMS:
                terms[channel], totals[to] = step(order, channel, halos[channel], totals[to])
            elif channel == 0:
                (totals[to],) = step(order, channel, halos[channel], totals[to])
            else:
                evolved, density = step(order, channel, halos[channel], totals[to], totals[1 - to])
        if order == 1:
            halos_in = halos
        if order == 2:
            _, spot = lax.optimization_barrier((terms[0], spot))
            half = f32(3 * planes // 2, rows, cells)
            keep, send = kernel(
                functools.partial(current_kernel, planes, rows, scale),
                "current_part", (half, half), 2, 6,
                [pltpu.VMEM((2, planes, rows + 16, cells), jnp.float32)],
            )(where, spot, first, second, *halos_in[0][1:], *halos_in[1][1:])
            got = lax.ppermute(send, "orb", [(i, (i // RUN ^ 1) * RUN + i % RUN) for i in range(orbs)])
            quarter = f32(3 * planes // 4, rows, cells)
            keep, send = kernel(merge_kernel, "merge_current", (quarter, quarter), 1, 2, [])(spot, keep, got)
            got = lax.ppermute(send, "orb", [(i, (i // RUN ^ 2) * RUN + i % RUN) for i in range(orbs)])

    fields = jnp.concatenate([density, keep + got], axis=0)
    fields = jnp.moveaxis(fields, 1, 0)
    fields = lax.all_to_all(fields, "orb", 0, 0, tiled=True)
    density, current = kernel(
        functools.partial(gather_kernel, planes),
        "sum_over_orb", (f32(planes, 1, cells), f32(3, planes, 1, cells)), 0, 1, [],
    )(fields)
    return evolved.reshape(orbitals.shape), density, current


def solution(mesh):
    in_specs = (P(None, "orb", "dom", None, None), P("dom", None, None), P(), P(), P(), P(), P())
    out_specs = (
        P(None, "orb", "dom", None, None),
        P("dom", "orb", None),
        P(None, "dom", "orb", None),
    )
    return jax.shard_map(body, mesh=mesh, in_specs=in_specs, out_specs=out_specs, check_vma=False)
```

```python
import functools

import jax
import jax.numpy as jnp
from jax import lax
from jax.experimental import pallas as pl
from jax.experimental.pallas import tpu as pltpu
from jax.sharding import PartitionSpec as P

TERMS = 4
BOX = 8
PROJ = 4
GROUP = 32
RUN = 3

spacing = 0.5
time_step = 0.05
second_taps = (-205.0 / 72.0, 8.0 / 5.0, -1.0 / 5.0, 8.0 / 315.0, -1.0 / 560.0)
first_taps = (0.0, 4.0 / 5.0, -1.0 / 5.0, 4.0 / 105.0, -1.0 / 280.0)
kinetic = tuple(-0.5 * tap / (spacing * spacing) for tap in second_taps)
slope = tuple(tap / spacing for tap in first_taps)

VMEM = pl.BlockSpec(memory_space=pltpu.VMEM)
SMEM = pl.BlockSpec(memory_space=pltpu.SMEM)
FAR = pl.BlockSpec(memory_space=pltpu.HBM)


def f32(*shape):
    return jax.ShapeDtypeStruct(shape, jnp.float32)


def shifted(value, offset):
    cells = value.shape[-1]
    lane = lax.broadcasted_iota(jnp.int32, value.shape, value.ndim - 1)
    inside = (lane < cells - offset) if offset > 0 else (lane >= -offset)
    return jnp.where(inside, pltpu.roll(value, (-offset) % cells, value.ndim - 1), 0.0)


def fill_padded(padded, planes, rows, read):
    cells = padded.shape[-1]
    for b in range(planes):
        padded[b, 0:8, :] = jnp.zeros((8, cells), jnp.float32)
        padded[b, 8 + rows : 16 + rows, :] = jnp.zeros((8, cells), jnp.float32)
        padded[b, 8 : 8 + rows, :] = read(b)


def atom_of(atoms, anchor, row, slot):
    atom = jnp.maximum(atoms[row, slot], 0)
    return anchor[1, atom], anchor[2, atom]


def fold(vectors):
    row = lax.broadcasted_iota(jnp.int32, vectors[0].shape, 0)
    for step in (4, 2, 1):
        lower = (row & step) == 0
        merged = []
        for a, b in zip(vectors[:step], vectors[step:]):
            crossed = jnp.where(lower, b, a)
            if step == 4:
                partner = pltpu.roll(crossed, 4, 0)
            else:
                partner = jnp.where(lower, pltpu.roll(crossed, 8 - step, 0), pltpu.roll(crossed, step, 0))
            merged.append(jnp.where(lower, a, b) + partner)
        vectors = merged
    return vectors[0]


def partial_sums(planes, rows, slots, me, atoms, anchor, u, proj, sums):
    cells = u.shape[-1]
    behind = jnp.maximum(me - 1, 0)

    def group(index, carry):
        stored = []
        for side, row in ((0, me), (1, behind)):
            for pair in range(GROUP // 2):
                products = []
                for slot in (index * GROUP + 2 * pair, index * GROUP + 2 * pair + 1):
                    y0, z0 = atom_of(atoms, anchor, row, slot)
                    shift = jnp.where(z0 == 0, 0, cells - z0)
                    boxes = [pltpu.roll(u[pl.ds(i * rows + y0, BOX), :], shift, 1) for i in range(planes)]
                    for p in range(PROJ):
                        first = p * BOX + side * planes
                        total = proj[first] * boxes[0]
                        for i in range(1, planes):
                            total = total + proj[first + i] * boxes[i]
                        products.append(total)
                at = side * slots * PROJ + index * GROUP * PROJ + 8 * pair
                stored.append((pl.multiple_of(at, 8), fold(products)))
        for at, value in stored:
            sums[pl.ds(at, 8), :] = value
        return carry

    lax.fori_loop(0, slots // GROUP, group, 0)
    size = slots * PROJ
    lines = [jnp.sum(sums[side * size : (side + 1) * size, :].T, axis=0, keepdims=True) for side in (0, 1)]
    return jnp.concatenate(lines + [jnp.zeros((6, size), jnp.float32)], axis=0)


def halo_weights(even, planes, taps, mirror):
    pair, other = {}, {}
    for i in range(planes):
        for j in range(planes):
            above = taps[planes + j - i] if j <= i else 0.0
            below = mirror * taps[planes + i - j] if i <= j else 0.0
            pair[i, j] = jnp.where(even, above, below)
            other[i, j] = jnp.where(even, below, above)
    return pair, other


def prepare_kernel(
    planes, rows, slots, where, atoms, anchor, strength, projector_far, u,
    proj, weight, message, sums, projector, sems,
):
    cells = u.shape[-1]
    size = planes * rows
    fetch = pltpu.make_async_copy(u.at[0], message.at[0:size], sems.at[0])
    fetch_projector = pltpu.make_async_copy(projector_far, projector, sems.at[1])
    fetch.start()
    fetch_projector.start()
    me = where[0]
    behind = jnp.maximum(me - 1, 0)
    lane = lax.broadcasted_iota(jnp.int32, (8, cells), 1)
    line = lax.broadcasted_iota(jnp.int32, (8, cells), 0)
    listed = jnp.zeros((8, cells), jnp.float32)
    for slot in range(slots):
        own = jnp.where(atoms[me, slot] >= 0, 1.0, 0.0)
        before = jnp.where((atoms[behind, slot] >= 0) & (me > 0), 1.0, 0.0)
        here = (lane // PROJ) == slot
        listed = jnp.where(here & (line == 0), own, jnp.where(here & (line == 1), before, listed))
    strengths = jnp.zeros((8, cells), jnp.float32)
    for p in range(PROJ):
        strengths = jnp.where((lane % PROJ) == p, strength[p], strengths)
    weight[...] = listed * strengths

    fetch_projector.wait()
    for chunk in range(BOX**3 // cells):
        block = projector[:, chunk * cells : (chunk + 1) * cells]
        for part in range(cells // BOX):
            i, j = chunk * (cells // BOX**2) + part // BOX, part % BOX
            moved = block if part == 0 else pltpu.roll(block, cells - part * BOX, 1)
            moved = jnp.where(lane[:PROJ] < BOX, moved, 0.0)
            for p in range(PROJ):
                proj[p * BOX + i, j : j + 1, :] = moved[p : p + 1]

    fetch.wait()
    message[size : size + 8, :] = partial_sums(planes, rows, slots, me, atoms, anchor, message, proj, sums)


def second_kernel(
    planes, rows, slots, domains, where, atoms, anchor, laser, potential, proj, u, v, message, sums, sem
):
    cells = u.shape[-1]
    size = planes * rows
    me = where[0]
    fetch = pltpu.make_async_copy(u.at[1], message.at[0:size], sem)
    fetch.start()
    y = lax.broadcasted_iota(jnp.int32, (rows, cells), 0).astype(jnp.float32)
    z = lax.broadcasted_iota(jnp.int32, (rows, cells), 1).astype(jnp.float32)
    along = laser[1] * ((y - (rows - 1) / 2.0) * spacing) + laser[2] * ((z - (cells - 1) / 2.0) * spacing)
    for i in range(planes):
        x = ((me * planes + i).astype(jnp.float32) - (domains * planes - 1) / 2.0) * spacing
        v[i] = potential[i] + laser[0] * x + along + 3.0 * kinetic[0]
    fetch.wait()
    message[size : size + 8, :] = partial_sums(planes, rows, slots, me, atoms, anchor, message, proj, sums)


def step_kernel(planes, rows, slots, factor, last, scale, *refs):
    where, atoms, anchor, u, other_u, pair_u, v, weight, proj, evolved, *refs = refs
    size = planes * rows
    if last == "both":
        held, result, density, acc, padded, spread, sums = refs
    elif last:
        result, acc, padded, spread, sums = refs
    else:
        message, result, acc, padded, spread, sums = refs
    cells = v.shape[-1]
    me = where[0]
    behind = jnp.maximum(me - 1, 0)
    even = lax.rem(me, 2) == 0
    pair_w, other_w = halo_weights(even, planes, kinetic, 1.0)

    def plane_of(ref, i):
        return ref[i * rows : (i + 1) * rows, :]

    fill_padded(padded, planes, rows, lambda i: plane_of(u, i))
    for i in range(planes):
        centre = plane_of(u, i)
        total = v[i] * centre
        for m in (1, 2, 3, 4):
            near = padded[i, 8 + m : 8 + m + rows, :] + padded[i, 8 - m : 8 - m + rows, :]
            near = near + shifted(centre, m) + shifted(centre, -m)
            if i + m < planes:
                near = near + plane_of(u, i + m)
            if i >= m:
                near = near + plane_of(u, i - m)
            total = total + kinetic[m] * near
        for j in range(planes):
            total = total + pair_w[i, j] * plane_of(pair_u, j) + other_w[i, j] * plane_of(other_u, j)
        acc[i * rows : (i + 1) * rows, :] = total

    mine, of_pair, of_other = (ref[size : size + 8, :] for ref in (u, pair_u, other_u))
    ahead = jnp.where(even, of_pair, of_other)
    back = jnp.where(even, of_other, of_pair)
    for side, got in ((0, ahead[1:2]), (1, back[0:1])):
        line = (mine[side : side + 1] + got) * weight[side : side + 1, :]
        spread[side * cells : (side + 1) * cells, :] = jnp.broadcast_to(line, (cells, cells)).T

    def group(index, carry):
        added = []
        for slot in [index * GROUP + k for k in range(GROUP)]:
            for side, row in ((0, me), (1, behind)):
                y0, z0 = atom_of(atoms, anchor, row, slot)
                at = side * slots * PROJ + slot * PROJ
                lines = [jnp.broadcast_to(spread[pl.ds(at + p, 1), :], (BOX, cells)) for p in range(PROJ)]
                for i in range(planes):
                    delta = lines[0] * proj[side * planes + i]
                    for p in range(1, PROJ):
                        delta = delta + lines[p] * proj[p * BOX + side * planes + i]
                    added.append((pl.ds(i * rows + y0, BOX), pltpu.roll(delta, z0, 1)))
        for at_rows, delta in added:
            acc[at_rows, :] = acc[at_rows, :] + delta
        return carry

    lax.fori_loop(0, slots // GROUP, group, 0)
    for i in range(planes):
        span = slice(i * rows, (i + 1) * rows)
        new = factor * acc[span, :]
        total = evolved[span, :] + new
        if last == "both":
            real = held[span, :]
            result[0, span, :] = real
            result[1, span, :] = total
            density[i] = scale * (real * real + total * total)
        else:
            result[span, :] = total
        if not last:
            message[span, :] = new
    if not last:
        message[size : size + 8, :] = partial_sums(planes, rows, slots, me, atoms, anchor, message, proj, sums)


def current_kernel(
    planes, rows, scale, where, spot, real, imag, real_other, real_pair, imag_other, imag_pair, keep, send, padded
):
    halos = ((real, real_pair, real_other), (imag, imag_pair, imag_other))
    pair_w, other_w = halo_weights(lax.rem(where[0], 2) == 0, planes, slope, -1.0)
    lower = lax.rem(spot[0], 2) == 0

    def plane_of(ref, i):
        return ref[i * rows : (i + 1) * rows, :]

    for ch in range(2):
        fill_padded(padded.at[ch], planes, rows, lambda i, ch=ch: plane_of(halos[ch][0], i))
    flows = {}
    for i in range(planes):
        gradients = []
        for ch in range(2):
            own, pair, other = halos[ch]
            centre = plane_of(own, i)
            along_x = along_y = along_z = 0.0
            for m in (1, 2, 3, 4):
                if i + m < planes:
                    along_x = along_x + slope[m] * plane_of(own, i + m)
                if i >= m:
                    along_x = along_x - slope[m] * plane_of(own, i - m)
                along_y = along_y + slope[m] * (
                    padded[ch, i, 8 + m : 8 + m + rows, :] - padded[ch, i, 8 - m : 8 - m + rows, :]
                )
                along_z = along_z + slope[m] * (shifted(centre, m) - shifted(centre, -m))
            for j in range(planes):
                along_x = along_x + pair_w[i, j] * plane_of(pair, j) + other_w[i, j] * plane_of(other, j)
            gradients.append((along_x, along_y, along_z))
        half = planes // 2
        for c in range(3):
            flow = scale * (plane_of(real, i) * gradients[1][c] - plane_of(imag, i) * gradients[0][c])
            at = c * half + i % half
            if i < half:
                keep[at] = flow
            else:
                first = keep[at]
                keep[at] = jnp.where(lower, first, flow)
                send[at] = jnp.where(lower, flow, first)


def merge_kernel(spot, held, got, keep, send):
    lower = lax.rem(spot[0] // 2, 2) == 0
    for c in range(3):
        first = held[2 * c] + got[2 * c]
        second = held[2 * c + 1] + got[2 * c + 1]
        keep[c] = jnp.where(lower, first, second)
        send[c] = jnp.where(lower, second, first)


def plane_kept(source):
    x = source // RUN
    return 2 * (x % 2) + x // 2 % 2


def gather_kernel(planes, got, density, current):
    totals = [None] * planes
    for source in range(got.shape[0]):
        p = plane_kept(source)
        totals[p] = got[source] if totals[p] is None else totals[p] + got[source]
    everywhere = totals[0] + totals[1] + totals[2] + totals[3]
    for i in range(planes):
        density[i] = everywhere[i : i + 1]
        for c in range(3):
            current[c, i] = totals[i][planes + c : planes + c + 1]


def body(orbitals, potential, laser_field, box_anchor, domain_atoms, projector, strength):
    planes, rows, cells = orbitals.shape[2:]
    size = planes * rows
    domains = lax.axis_size("dom")
    orbs = lax.axis_size("orb")
    slots = domain_atoms.shape[1]
    me = lax.axis_index("dom")
    where = me.reshape(1).astype(jnp.int32)
    places = (where, domain_atoms, box_anchor)
    spot = (lax.axis_index("orb") // RUN).reshape(1).astype(jnp.int32)
    scale = 2.0 / orbs

    pairs = [(i, i ^ 1) for i in range(domains)]
    others = [(i, i + 1) for i in range(1, domains - 1, 2)] + [(i + 1, i) for i in range(1, domains - 1, 2)]

    def exchange(value):
        other = lax.ppermute(value, "dom", others)
        return other, lax.ppermute(value, "dom", pairs)

    def kernel(function, name, out, scalars, arrays, scratch, far=0):
        return pl.pallas_call(
            function,
            out_shape=out,
            in_specs=[SMEM] * scalars + [VMEM] * arrays + [FAR] * far,
            out_specs=jax.tree.map(lambda _: VMEM, out),
            scratch_shapes=scratch,
            compiler_params=pltpu.CompilerParams(vmem_limit_bytes=32 * 1024 * 1024),
            cost_estimate=pl.CostEstimate(flops=8_000_000, bytes_accessed=10_000_000, transcendentals=0),
            name=name,
        )

    sums = pltpu.VMEM((2 * slots * PROJ, cells), jnp.float32)
    u = orbitals.reshape(2, size, cells)
    proj, weight, first = kernel(
        functools.partial(prepare_kernel, planes, rows, slots),
        "prepare_real",
        (f32(PROJ * BOX, BOX, cells), f32(8, cells), f32(size + 8, cells)),
        4, 0,
        [sums, pltpu.VMEM((PROJ, BOX**3), jnp.float32), pltpu.SemaphoreType.DMA((2,))],
        2,
    )(*places, strength, projector, u)
    v, second = kernel(
        functools.partial(second_kernel, planes, rows, slots, domains),
        "prepare_imag",
        (f32(planes, rows, cells), f32(size + 8, cells)),
        4, 2, [sums, pltpu.SemaphoreType.DMA], 1,
    )(*places, laser_field, potential, proj, u)

    def step(order, channel, halos, evolved, held=None):
        sign = 1.0 if (channel + order) % 2 == 0 else -1.0
        last = False if order < TERMS else ("both" if held is not None else True)
        out = (f32(size, cells),)
        if not last:
            out = (f32(size + 8, cells),) + out
        if last == "both":
            out = (f32(2, size, cells), f32(planes, rows, cells))
        extra = () if held is None else (held,)
        return kernel(
            functools.partial(step_kernel, planes, rows, slots, sign * time_step / order, last, scale),
            "taylor_step", out, 3, 7 + len(extra),
            [
                pltpu.VMEM((size, cells), jnp.float32),
                pltpu.VMEM((planes, rows + 16, cells), jnp.float32),
                pltpu.VMEM((2 * slots * PROJ, cells), jnp.float32),
                sums,
            ],
        )(*places, *halos, v, weight, proj, evolved, *extra)

    terms = [first, second]
    totals = [first, second]
    for order in range(1, TERMS + 1):
        halos = [(term, *exchange(term)) for term in terms]
        if order == 1:
            first_halos = (first, second, *halos[0][1:], *halos[1][1:])
        if order == 2:
            halo, spot = lax.optimization_barrier((halos[0][1], spot))
            halos[0] = (halos[0][0], halo, halos[0][2])
            half = f32(3 * planes // 2, rows, cells)
            keep, send = kernel(
                functools.partial(current_kernel, planes, rows, scale),
                "current_part", (half, half), 2, 6,
                [pltpu.VMEM((2, planes, rows + 16, cells), jnp.float32)],
            )(where, spot, *first_halos)
            got = lax.ppermute(send, "orb", [(i, (i // RUN ^ 1) * RUN + i % RUN) for i in range(orbs)])
        if order == 3:
            halo, spot = lax.optimization_barrier((halos[0][1], spot))
            halos[0] = (halos[0][0], halo, halos[0][2])
            quarter = f32(3 * planes // 4, rows, cells)
            keep, send = kernel(merge_kernel, "merge_current", (quarter, quarter), 1, 2, [])(spot, keep, got)
            got = lax.ppermute(send, "orb", [(i, (i // RUN ^ 2) * RUN + i % RUN) for i in range(orbs)])
        for channel in (0, 1):
            to = (channel + order) % 2
            if order < TERMS:
                terms[channel], totals[to] = step(order, channel, halos[channel], totals[to])
            elif channel == 0:
                (totals[to],) = step(order, channel, halos[channel], totals[to])
            else:
                evolved, density = step(order, channel, halos[channel], totals[to], totals[1 - to])

    fields = jnp.concatenate([density, keep + got], axis=0)
    fields = jnp.moveaxis(fields, 1, 0)
    fields = lax.all_to_all(fields, "orb", 0, 0, tiled=True)
    density, current = kernel(
        functools.partial(gather_kernel, planes),
        "sum_over_orb", (f32(planes, 1, cells), f32(3, planes, 1, cells)), 0, 1, [],
    )(fields)
    return evolved.reshape(orbitals.shape), density, current


def solution(mesh):
    in_specs = (P(None, "orb", "dom", None, None), P("dom", None, None), P(), P(), P(), P(), P())
    out_specs = (
        P(None, "orb", "dom", None, None),
        P("dom", "orb", None),
        P(None, "dom", "orb", None),
    )
    return jax.shard_map(body, mesh=mesh, in_specs=in_specs, out_specs=out_specs, check_vma=False)
```

```python
import functools

import jax
import jax.numpy as jnp
from jax import lax
from jax.experimental import pallas as pl
from jax.experimental.pallas import tpu as pltpu
from jax.sharding import PartitionSpec as P

TERMS = 4
BOX = 8
PROJ = 4
GROUP = 32
RUN = 3

spacing = 0.5
time_step = 0.05
second_taps = (-205.0 / 72.0, 8.0 / 5.0, -1.0 / 5.0, 8.0 / 315.0, -1.0 / 560.0)
first_taps = (0.0, 4.0 / 5.0, -1.0 / 5.0, 4.0 / 105.0, -1.0 / 280.0)
kinetic = tuple(-0.5 * tap / (spacing * spacing) for tap in second_taps)
slope = tuple(tap / spacing for tap in first_taps)

VMEM = pl.BlockSpec(memory_space=pltpu.VMEM)
SMEM = pl.BlockSpec(memory_space=pltpu.SMEM)


def f32(*shape):
    return jax.ShapeDtypeStruct(shape, jnp.float32)


def shifted(value, offset):
    cells = value.shape[-1]
    lane = lax.broadcasted_iota(jnp.int32, value.shape, value.ndim - 1)
    inside = (lane < cells - offset) if offset > 0 else (lane >= -offset)
    return jnp.where(inside, pltpu.roll(value, (-offset) % cells, value.ndim - 1), 0.0)


def fill_padded(padded, planes, rows, read):
    cells = padded.shape[-1]
    for b in range(planes):
        padded[b, 0:8, :] = jnp.zeros((8, cells), jnp.float32)
        padded[b, 8 + rows : 16 + rows, :] = jnp.zeros((8, cells), jnp.float32)
        padded[b, 8 : 8 + rows, :] = read(b)


def atom_of(atoms, anchor, row, slot):
    atom = jnp.maximum(atoms[row, slot], 0)
    return anchor[1, atom], anchor[2, atom]


def fold(vectors):
    row = lax.broadcasted_iota(jnp.int32, vectors[0].shape, 0)
    for step in (4, 2, 1):
        lower = (row & step) == 0
        merged = []
        for a, b in zip(vectors[:step], vectors[step:]):
            crossed = jnp.where(lower, b, a)
            if step == 4:
                partner = pltpu.roll(crossed, 4, 0)
            else:
                partner = jnp.where(lower, pltpu.roll(crossed, 8 - step, 0), pltpu.roll(crossed, step, 0))
            merged.append(jnp.where(lower, a, b) + partner)
        vectors = merged
    return vectors[0]


def partial_sums(planes, rows, slots, me, atoms, anchor, u, proj, sums):
    cells = u.shape[-1]
    behind = jnp.maximum(me - 1, 0)

    def group(index, carry):
        stored = []
        for side, row in ((0, me), (1, behind)):
            for pair in range(GROUP // 2):
                products = []
                for slot in (index * GROUP + 2 * pair, index * GROUP + 2 * pair + 1):
                    y0, z0 = atom_of(atoms, anchor, row, slot)
                    shift = jnp.where(z0 == 0, 0, cells - z0)
                    boxes = [pltpu.roll(u[pl.ds(i * rows + y0, BOX), :], shift, 1) for i in range(planes)]
                    for p in range(PROJ):
                        first = p * BOX + side * planes
                        total = proj[first] * boxes[0]
                        for i in range(1, planes):
                            total = total + proj[first + i] * boxes[i]
                        products.append(total)
                at = side * slots * PROJ + index * GROUP * PROJ + 8 * pair
                stored.append((pl.multiple_of(at, 8), fold(products)))
        for at, value in stored:
            sums[pl.ds(at, 8), :] = value
        return carry

    lax.fori_loop(0, slots // GROUP, group, 0)
    size = slots * PROJ
    lines = [jnp.sum(sums[side * size : (side + 1) * size, :].T, axis=0, keepdims=True) for side in (0, 1)]
    return jnp.concatenate(lines + [jnp.zeros((6, size), jnp.float32)], axis=0)


def halo_weights(even, planes, taps, mirror):
    pair, other = {}, {}
    for i in range(planes):
        for j in range(planes):
            above = taps[planes + j - i] if j <= i else 0.0
            below = mirror * taps[planes + i - j] if i <= j else 0.0
            pair[i, j] = jnp.where(even, above, below)
            other[i, j] = jnp.where(even, below, above)
    return pair, other


def prepare_kernel(
    planes, rows, slots, where, atoms, anchor, strength, projector, u,
    proj, weight, message, sums,
):
    cells = u.shape[-1]
    size = planes * rows
    me = where[0]
    behind = jnp.maximum(me - 1, 0)
    lane = lax.broadcasted_iota(jnp.int32, (8, cells), 1)
    line = lax.broadcasted_iota(jnp.int32, (8, cells), 0)
    listed = jnp.zeros((8, cells), jnp.float32)
    for slot in range(slots):
        own = jnp.where(atoms[me, slot] >= 0, 1.0, 0.0)
        before = jnp.where((atoms[behind, slot] >= 0) & (me > 0), 1.0, 0.0)
        here = (lane // PROJ) == slot
        listed = jnp.where(here & (line == 0), own, jnp.where(here & (line == 1), before, listed))
    strengths = jnp.zeros((8, cells), jnp.float32)
    for p in range(PROJ):
        strengths = jnp.where((lane % PROJ) == p, strength[p], strengths)
    weight[...] = listed * strengths

    for chunk in range(BOX**3 // cells):
        block = projector[:, chunk * cells : (chunk + 1) * cells]
        for part in range(cells // BOX):
            i, j = chunk * (cells // BOX**2) + part // BOX, part % BOX
            moved = block if part == 0 else pltpu.roll(block, cells - part * BOX, 1)
            moved = jnp.where(lane[:PROJ] < BOX, moved, 0.0)
            for p in range(PROJ):
                proj[p * BOX + i, j : j + 1, :] = moved[p : p + 1]

    message[0:size, :] = u[0]
    message[size : size + 8, :] = partial_sums(planes, rows, slots, me, atoms, anchor, u.at[0], proj, sums)


def second_kernel(
    planes, rows, slots, domains, where, atoms, anchor, laser, potential, proj, u, v, message, sums
):
    cells = u.shape[-1]
    size = planes * rows
    me = where[0]
    y = lax.broadcasted_iota(jnp.int32, (rows, cells), 0).astype(jnp.float32)
    z = lax.broadcasted_iota(jnp.int32, (rows, cells), 1).astype(jnp.float32)
    along = laser[1] * ((y - (rows - 1) / 2.0) * spacing) + laser[2] * ((z - (cells - 1) / 2.0) * spacing)
    for i in range(planes):
        x = ((me * planes + i).astype(jnp.float32) - (domains * planes - 1) / 2.0) * spacing
        v[i] = potential[i] + laser[0] * x + along + 3.0 * kinetic[0]
    message[0:size, :] = u[1]
    message[size : size + 8, :] = partial_sums(planes, rows, slots, me, atoms, anchor, u.at[1], proj, sums)


def step_kernel(planes, rows, slots, factor, last, scale, *refs):
    where, atoms, anchor, u, other_u, pair_u, v, weight, proj, evolved, *refs = refs
    size = planes * rows
    if last == "both":
        held, result, density, acc, padded, spread, sums = refs
    elif last:
        result, acc, padded, spread, sums = refs
    else:
        message, result, acc, padded, spread, sums = refs
    cells = v.shape[-1]
    me = where[0]
    behind = jnp.maximum(me - 1, 0)
    even = lax.rem(me, 2) == 0
    pair_w, other_w = halo_weights(even, planes, kinetic, 1.0)

    def plane_of(ref, i):
        return ref[i * rows : (i + 1) * rows, :]

    fill_padded(padded, planes, rows, lambda i: plane_of(u, i))
    for i in range(planes):
        centre = plane_of(u, i)
        total = v[i] * centre
        for m in (1, 2, 3, 4):
            near = padded[i, 8 + m : 8 + m + rows, :] + padded[i, 8 - m : 8 - m + rows, :]
            near = near + shifted(centre, m) + shifted(centre, -m)
            if i + m < planes:
                near = near + plane_of(u, i + m)
            if i >= m:
                near = near + plane_of(u, i - m)
            total = total + kinetic[m] * near
        for j in range(planes):
            total = total + pair_w[i, j] * plane_of(pair_u, j) + other_w[i, j] * plane_of(other_u, j)
        acc[i * rows : (i + 1) * rows, :] = total

    mine, of_pair, of_other = (ref[size : size + 8, :] for ref in (u, pair_u, other_u))
    ahead = jnp.where(even, of_pair, of_other)
    back = jnp.where(even, of_other, of_pair)
    for side, got in ((0, ahead[1:2]), (1, back[0:1])):
        line = (mine[side : side + 1] + got) * weight[side : side + 1, :]
        spread[side * cells : (side + 1) * cells, :] = jnp.broadcast_to(line, (cells, cells)).T

    def group(index, carry):
        added = []
        for slot in [index * GROUP + k for k in range(GROUP)]:
            for side, row in ((0, me), (1, behind)):
                y0, z0 = atom_of(atoms, anchor, row, slot)
                at = side * slots * PROJ + slot * PROJ
                lines = [jnp.broadcast_to(spread[pl.ds(at + p, 1), :], (BOX, cells)) for p in range(PROJ)]
                for i in range(planes):
                    delta = lines[0] * proj[side * planes + i]
                    for p in range(1, PROJ):
                        delta = delta + lines[p] * proj[p * BOX + side * planes + i]
                    added.append((pl.ds(i * rows + y0, BOX), pltpu.roll(delta, z0, 1)))
        for at_rows, delta in added:
            acc[at_rows, :] = acc[at_rows, :] + delta
        return carry

    lax.fori_loop(0, slots // GROUP, group, 0)
    for i in range(planes):
        span = slice(i * rows, (i + 1) * rows)
        new = factor * acc[span, :]
        total = evolved[span, :] + new
        if last == "both":
            real = held[span, :]
            result[0, span, :] = real
            result[1, span, :] = total
            density[i] = scale * (real * real + total * total)
        else:
            result[span, :] = total
        if not last:
            message[span, :] = new
    if not last:
        message[size : size + 8, :] = partial_sums(planes, rows, slots, me, atoms, anchor, message, proj, sums)


def current_kernel(
    planes, rows, scale, where, spot, real, imag, real_other, real_pair, imag_other, imag_pair, keep, send, padded
):
    halos = ((real, real_pair, real_other), (imag, imag_pair, imag_other))
    pair_w, other_w = halo_weights(lax.rem(where[0], 2) == 0, planes, slope, -1.0)
    lower = lax.rem(spot[0], 2) == 0

    def plane_of(ref, i):
        return ref[i * rows : (i + 1) * rows, :]

    for ch in range(2):
        fill_padded(padded.at[ch], planes, rows, lambda i, ch=ch: plane_of(halos[ch][0], i))
    flows = {}
    for i in range(planes):
        gradients = []
        for ch in range(2):
            own, pair, other = halos[ch]
            centre = plane_of(own, i)
            along_x = along_y = along_z = 0.0
            for m in (1, 2, 3, 4):
                if i + m < planes:
                    along_x = along_x + slope[m] * plane_of(own, i + m)
                if i >= m:
                    along_x = along_x - slope[m] * plane_of(own, i - m)
                along_y = along_y + slope[m] * (
                    padded[ch, i, 8 + m : 8 + m + rows, :] - padded[ch, i, 8 - m : 8 - m + rows, :]
                )
                along_z = along_z + slope[m] * (shifted(centre, m) - shifted(centre, -m))
            for j in range(planes):
                along_x = along_x + pair_w[i, j] * plane_of(pair, j) + other_w[i, j] * plane_of(other, j)
            gradients.append((along_x, along_y, along_z))
        half = planes // 2
        for c in range(3):
            flow = scale * (plane_of(real, i) * gradients[1][c] - plane_of(imag, i) * gradients[0][c])
            at = c * half + i % half
            if i < half:
                keep[at] = flow
            else:
                first = keep[at]
                keep[at] = jnp.where(lower, first, flow)
                send[at] = jnp.where(lower, flow, first)


def gather_kernel(planes, got, density, current):
    half = planes // 2
    totals = [None, None]
    for source in range(got.shape[0]):
        kept = source // RUN % 2
        totals[kept] = got[source] if totals[kept] is None else totals[kept] + got[source]
    everywhere = totals[0] + totals[1]
    for i in range(planes):
        density[i] = everywhere[i : i + 1]
        for c in range(3):
            at = planes + c * half + i % half
            current[c, i] = totals[i // half][at : at + 1]


def body(orbitals, potential, laser_field, box_anchor, domain_atoms, projector, strength):
    planes, rows, cells = orbitals.shape[2:]
    size = planes * rows
    domains = lax.axis_size("dom")
    orbs = lax.axis_size("orb")
    slots = domain_atoms.shape[1]
    me = lax.axis_index("dom")
    where = me.reshape(1).astype(jnp.int32)
    places = (where, domain_atoms, box_anchor)
    spot = (lax.axis_index("orb") // RUN).reshape(1).astype(jnp.int32)
    scale = 2.0 / orbs

    pairs = [(i, i ^ 1) for i in range(domains)]
    others = [(i, i + 1) for i in range(1, domains - 1, 2)] + [(i + 1, i) for i in range(1, domains - 1, 2)]

    def exchange(value):
        other = lax.ppermute(value, "dom", others)
        return other, lax.ppermute(value, "dom", pairs)

    def kernel(function, name, out, scalars, arrays, scratch):
        return pl.pallas_call(
            function,
            out_shape=out,
            in_specs=[SMEM] * scalars + [VMEM] * arrays,
            out_specs=jax.tree.map(lambda _: VMEM, out),
            scratch_shapes=scratch,
            compiler_params=pltpu.CompilerParams(vmem_limit_bytes=32 * 1024 * 1024),
            cost_estimate=pl.CostEstimate(flops=8_000_000, bytes_accessed=10_000_000, transcendentals=0),
            name=name,
        )

    sums = pltpu.VMEM((2 * slots * PROJ, cells), jnp.float32)
    u = orbitals.reshape(2, size, cells)
    proj, weight, first = kernel(
        functools.partial(prepare_kernel, planes, rows, slots),
        "prepare_real",
        (f32(PROJ * BOX, BOX, cells), f32(8, cells), f32(size + 8, cells)),
        4, 2, [sums],
    )(*places, strength, projector, u)
    v, second = kernel(
        functools.partial(second_kernel, planes, rows, slots, domains),
        "prepare_imag",
        (f32(planes, rows, cells), f32(size + 8, cells)),
        4, 3, [sums],
    )(*places, laser_field, potential, proj, u)

    def step(order, channel, halos, evolved, held=None):
        sign = 1.0 if (channel + order) % 2 == 0 else -1.0
        last = False if order < TERMS else ("both" if held is not None else True)
        out = (f32(size, cells),)
        if not last:
            out = (f32(size + 8, cells),) + out
        if last == "both":
            out = (f32(2, size, cells), f32(planes, rows, cells))
        extra = () if held is None else (held,)
        return kernel(
            functools.partial(step_kernel, planes, rows, slots, sign * time_step / order, last, scale),
            "taylor_step", out, 3, 7 + len(extra),
            [
                pltpu.VMEM((size, cells), jnp.float32),
                pltpu.VMEM((planes, rows + 16, cells), jnp.float32),
                pltpu.VMEM((2 * slots * PROJ, cells), jnp.float32),
                sums,
            ],
        )(*places, *halos, v, weight, proj, evolved, *extra)

    terms = [first, second]
    totals = [first, second]
    for order in range(1, TERMS + 1):
        halos = [(term, *exchange(term)) for term in terms]
        if order == TERMS:
            half = f32(3 * planes // 2, rows, cells)
            keep, send = kernel(
                functools.partial(current_kernel, planes, rows, scale),
                "current_part", (half, half), 2, 6,
                [pltpu.VMEM((2, planes, rows + 16, cells), jnp.float32)],
            )(where, spot, *first_halos)
            got = lax.ppermute(send, "orb", [(i, (i // RUN ^ 1) * RUN + i % RUN) for i in range(orbs)])
        for channel in (0, 1):
            to = (channel + order) % 2
            if order < TERMS:
                terms[channel], totals[to] = step(order, channel, halos[channel], totals[to])
            elif channel == 0:
                (totals[to],) = step(order, channel, halos[channel], totals[to])
            else:
                evolved, density = step(order, channel, halos[channel], totals[to], totals[1 - to])
        if order == 1:
            first_halos = (first, second, *halos[0][1:], *halos[1][1:])

    fields = jnp.concatenate([density, keep + got], axis=0)
    fields = jnp.moveaxis(fields, 1, 0)
    fields = lax.all_to_all(fields, "orb", 0, 0, tiled=True)
    density, current = kernel(
        functools.partial(gather_kernel, planes),
        "sum_over_orb", (f32(planes, 1, cells), f32(3, planes, 1, cells)), 0, 1, [],
    )(fields)
    return evolved.reshape(orbitals.shape), density, current


def solution(mesh):
    in_specs = (P(None, "orb", "dom", None, None), P("dom", None, None), P(), P(), P(), P(), P())
    out_specs = (
        P(None, "orb", "dom", None, None),
        P("dom", "orb", None),
        P(None, "dom", "orb", None),
    )
    return jax.shard_map(body, mesh=mesh, in_specs=in_specs, out_specs=out_specs, check_vma=False)
```

```python
import functools

import jax
import jax.numpy as jnp
from jax import lax
from jax.experimental import pallas as pl
from jax.experimental.pallas import tpu as pltpu
from jax.sharding import PartitionSpec as P

TERMS = 4
BOX = 8
PROJ = 4
GROUP = 32
RUN = 3

spacing = 0.5
time_step = 0.05
second_taps = (-205.0 / 72.0, 8.0 / 5.0, -1.0 / 5.0, 8.0 / 315.0, -1.0 / 560.0)
first_taps = (0.0, 4.0 / 5.0, -1.0 / 5.0, 4.0 / 105.0, -1.0 / 280.0)
kinetic = tuple(-0.5 * tap / (spacing * spacing) for tap in second_taps)
slope = tuple(tap / spacing for tap in first_taps)

VMEM = pl.BlockSpec(memory_space=pltpu.VMEM)
SMEM = pl.BlockSpec(memory_space=pltpu.SMEM)


def f32(*shape):
    return jax.ShapeDtypeStruct(shape, jnp.float32)


def shifted(value, offset):
    cells = value.shape[-1]
    lane = lax.broadcasted_iota(jnp.int32, value.shape, value.ndim - 1)
    inside = (lane < cells - offset) if offset > 0 else (lane >= -offset)
    return jnp.where(inside, pltpu.roll(value, (-offset) % cells, value.ndim - 1), 0.0)


def fill_padded(padded, planes, rows, read):
    cells = padded.shape[-1]
    for b in range(planes):
        padded[b, 0:8, :] = jnp.zeros((8, cells), jnp.float32)
        padded[b, 8 + rows : 16 + rows, :] = jnp.zeros((8, cells), jnp.float32)
        padded[b, 8 : 8 + rows, :] = read(b)


def atom_of(atoms, anchor, row, slot):
    atom = jnp.maximum(atoms[row, slot], 0)
    return anchor[1, atom], anchor[2, atom]


def fold(vectors):
    row = lax.broadcasted_iota(jnp.int32, vectors[0].shape, 0)
    for step in (4, 2, 1):
        lower = (row & step) == 0
        merged = []
        for a, b in zip(vectors[:step], vectors[step:]):
            crossed = jnp.where(lower, b, a)
            if step == 4:
                partner = pltpu.roll(crossed, 4, 0)
            else:
                partner = jnp.where(lower, pltpu.roll(crossed, 8 - step, 0), pltpu.roll(crossed, step, 0))
            merged.append(jnp.where(lower, a, b) + partner)
        vectors = merged
    return vectors[0]


def partial_sums(planes, rows, slots, me, atoms, anchor, u, proj, sums):
    cells = u.shape[-1]
    behind = jnp.maximum(me - 1, 0)

    def group(index, carry):
        stored = []
        for side, row in ((0, me), (1, behind)):
            for pair in range(GROUP // 2):
                products = []
                for slot in (index * GROUP + 2 * pair, index * GROUP + 2 * pair + 1):
                    y0, z0 = atom_of(atoms, anchor, row, slot)
                    shift = jnp.where(z0 == 0, 0, cells - z0)
                    boxes = [pltpu.roll(u[pl.ds(i * rows + y0, BOX), :], shift, 1) for i in range(planes)]
                    for p in range(PROJ):
                        first = p * BOX + side * planes
                        total = proj[first] * boxes[0]
                        for i in range(1, planes):
                            total = total + proj[first + i] * boxes[i]
                        products.append(total)
                at = side * slots * PROJ + index * GROUP * PROJ + 8 * pair
                stored.append((pl.multiple_of(at, 8), fold(products)))
        for at, value in stored:
            sums[pl.ds(at, 8), :] = value
        return carry

    lax.fori_loop(0, slots // GROUP, group, 0)
    size = slots * PROJ
    lines = [jnp.sum(sums[side * size : (side + 1) * size, :].T, axis=0, keepdims=True) for side in (0, 1)]
    return jnp.concatenate(lines + [jnp.zeros((6, size), jnp.float32)], axis=0)


def halo_weights(even, planes, taps, mirror):
    pair, other = {}, {}
    for i in range(planes):
        for j in range(planes):
            above = taps[planes + j - i] if j <= i else 0.0
            below = mirror * taps[planes + i - j] if i <= j else 0.0
            pair[i, j] = jnp.where(even, above, below)
            other[i, j] = jnp.where(even, below, above)
    return pair, other


def prepare_kernel(
    planes, rows, slots, where, atoms, anchor, strength, projector, u,
    proj, weight, message, sums,
):
    cells = u.shape[-1]
    size = planes * rows
    me = where[0]
    behind = jnp.maximum(me - 1, 0)
    lane = lax.broadcasted_iota(jnp.int32, (8, cells), 1)
    line = lax.broadcasted_iota(jnp.int32, (8, cells), 0)
    listed = jnp.zeros((8, cells), jnp.float32)
    for slot in range(slots):
        own = jnp.where(atoms[me, slot] >= 0, 1.0, 0.0)
        before = jnp.where((atoms[behind, slot] >= 0) & (me > 0), 1.0, 0.0)
        here = (lane // PROJ) == slot
        listed = jnp.where(here & (line == 0), own, jnp.where(here & (line == 1), before, listed))
    strengths = jnp.zeros((8, cells), jnp.float32)
    for p in range(PROJ):
        strengths = jnp.where((lane % PROJ) == p, strength[p], strengths)
    weight[...] = listed * strengths

    for chunk in range(BOX**3 // cells):
        block = projector[:, chunk * cells : (chunk + 1) * cells]
        for part in range(cells // BOX):
            i, j = chunk * (cells // BOX**2) + part // BOX, part % BOX
            moved = block if part == 0 else pltpu.roll(block, cells - part * BOX, 1)
            moved = jnp.where(lane[:PROJ] < BOX, moved, 0.0)
            for p in range(PROJ):
                proj[p * BOX + i, j : j + 1, :] = moved[p : p + 1]

    message[0:size, :] = u[0]
    message[size : size + 8, :] = partial_sums(planes, rows, slots, me, atoms, anchor, u.at[0], proj, sums)


def second_kernel(
    planes, rows, slots, domains, where, atoms, anchor, laser, potential, proj, u, v, message, sums
):
    cells = u.shape[-1]
    size = planes * rows
    me = where[0]
    y = lax.broadcasted_iota(jnp.int32, (rows, cells), 0).astype(jnp.float32)
    z = lax.broadcasted_iota(jnp.int32, (rows, cells), 1).astype(jnp.float32)
    along = laser[1] * ((y - (rows - 1) / 2.0) * spacing) + laser[2] * ((z - (cells - 1) / 2.0) * spacing)
    for i in range(planes):
        x = ((me * planes + i).astype(jnp.float32) - (domains * planes - 1) / 2.0) * spacing
        v[i] = potential[i] + laser[0] * x + along + 3.0 * kinetic[0]
    message[0:size, :] = u[1]
    message[size : size + 8, :] = partial_sums(planes, rows, slots, me, atoms, anchor, u.at[1], proj, sums)


def local_part(planes, rows, i, u, v, padded):
    def plane_of(j):
        return u[j * rows : (j + 1) * rows, :]

    centre = plane_of(i)
    total = v[i] * centre
    for m in (1, 2, 3, 4):
        near = padded[i, 8 + m : 8 + m + rows, :] + padded[i, 8 - m : 8 - m + rows, :]
        near = near + shifted(centre, m) + shifted(centre, -m)
        if i + m < planes:
            near = near + plane_of(i + m)
        if i >= m:
            near = near + plane_of(i - m)
        total = total + kinetic[m] * near
    return total


def local_kernel(planes, rows, u, v, local, padded):
    fill_padded(padded, planes, rows, lambda i: u[i * rows : (i + 1) * rows, :])
    for i in range(planes):
        local[i * rows : (i + 1) * rows, :] = local_part(planes, rows, i, u, v, padded)


def step_kernel(planes, rows, slots, factor, last, scale, *refs):
    where, atoms, anchor, u, other_u, pair_u, v, weight, proj, evolved, *refs = refs
    size = planes * rows
    if last == "both":
        held, local, result, density, acc, padded, spread, sums = refs
    elif last:
        result, acc, padded, spread, sums = refs
    else:
        message, result, acc, padded, spread, sums = refs
    cells = v.shape[-1]
    me = where[0]
    behind = jnp.maximum(me - 1, 0)
    even = lax.rem(me, 2) == 0
    pair_w, other_w = halo_weights(even, planes, kinetic, 1.0)

    def plane_of(ref, i):
        return ref[i * rows : (i + 1) * rows, :]

    if last != "both":
        fill_padded(padded, planes, rows, lambda i: plane_of(u, i))
    for i in range(planes):
        total = plane_of(local, i) if last == "both" else local_part(planes, rows, i, u, v, padded)
        for j in range(planes):
            total = total + pair_w[i, j] * plane_of(pair_u, j) + other_w[i, j] * plane_of(other_u, j)
        acc[i * rows : (i + 1) * rows, :] = total

    mine, of_pair, of_other = (ref[size : size + 8, :] for ref in (u, pair_u, other_u))
    ahead = jnp.where(even, of_pair, of_other)
    back = jnp.where(even, of_other, of_pair)
    for side, got in ((0, ahead[1:2]), (1, back[0:1])):
        line = (mine[side : side + 1] + got) * weight[side : side + 1, :]
        spread[side * cells : (side + 1) * cells, :] = jnp.broadcast_to(line, (cells, cells)).T

    def group(index, carry):
        added = []
        for slot in [index * GROUP + k for k in range(GROUP)]:
            for side, row in ((0, me), (1, behind)):
                y0, z0 = atom_of(atoms, anchor, row, slot)
                at = side * slots * PROJ + slot * PROJ
                lines = [jnp.broadcast_to(spread[pl.ds(at + p, 1), :], (BOX, cells)) for p in range(PROJ)]
                for i in range(planes):
                    delta = lines[0] * proj[side * planes + i]
                    for p in range(1, PROJ):
                        delta = delta + lines[p] * proj[p * BOX + side * planes + i]
                    added.append((pl.ds(i * rows + y0, BOX), pltpu.roll(delta, z0, 1)))
        for at_rows, delta in added:
            acc[at_rows, :] = acc[at_rows, :] + delta
        return carry

    lax.fori_loop(0, slots // GROUP, group, 0)
    for i in range(planes):
        span = slice(i * rows, (i + 1) * rows)
        new = factor * acc[span, :]
        total = evolved[span, :] + new
        if last == "both":
            real = held[span, :]
            result[0, span, :] = real
            result[1, span, :] = total
            density[i] = scale * (real * real + total * total)
        else:
            result[span, :] = total
        if not last:
            message[span, :] = new
    if not last:
        message[size : size + 8, :] = partial_sums(planes, rows, slots, me, atoms, anchor, message, proj, sums)


def current_kernel(
    planes, rows, scale, where, spot, real, imag, real_other, real_pair, imag_other, imag_pair, keep, send, padded
):
    halos = ((real, real_pair, real_other), (imag, imag_pair, imag_other))
    pair_w, other_w = halo_weights(lax.rem(where[0], 2) == 0, planes, slope, -1.0)
    lower = lax.rem(spot[0], 2) == 0

    def plane_of(ref, i):
        return ref[i * rows : (i + 1) * rows, :]

    for ch in range(2):
        fill_padded(padded.at[ch], planes, rows, lambda i, ch=ch: plane_of(halos[ch][0], i))
    flows = {}
    for i in range(planes):
        gradients = []
        for ch in range(2):
            own, pair, other = halos[ch]
            centre = plane_of(own, i)
            along_x = along_y = along_z = 0.0
            for m in (1, 2, 3, 4):
                if i + m < planes:
                    along_x = along_x + slope[m] * plane_of(own, i + m)
                if i >= m:
                    along_x = along_x - slope[m] * plane_of(own, i - m)
                along_y = along_y + slope[m] * (
                    padded[ch, i, 8 + m : 8 + m + rows, :] - padded[ch, i, 8 - m : 8 - m + rows, :]
                )
                along_z = along_z + slope[m] * (shifted(centre, m) - shifted(centre, -m))
            for j in range(planes):
                along_x = along_x + pair_w[i, j] * plane_of(pair, j) + other_w[i, j] * plane_of(other, j)
            gradients.append((along_x, along_y, along_z))
        half = planes // 2
        for c in range(3):
            flow = scale * (plane_of(real, i) * gradients[1][c] - plane_of(imag, i) * gradients[0][c])
            at = c * half + i % half
            if i < half:
                keep[at] = flow
            else:
                first = keep[at]
                keep[at] = jnp.where(lower, first, flow)
                send[at] = jnp.where(lower, flow, first)


def merge_kernel(spot, held, got, keep, send):
    lower = lax.rem(spot[0] // 2, 2) == 0
    for c in range(3):
        first = held[2 * c] + got[2 * c]
        second = held[2 * c + 1] + got[2 * c + 1]
        keep[c] = jnp.where(lower, first, second)
        send[c] = jnp.where(lower, second, first)


def plane_kept(source):
    x = source // RUN
    return 2 * (x % 2) + x // 2 % 2


def gather_kernel(planes, got, density, current):
    totals = [None] * planes
    for source in range(got.shape[0]):
        p = plane_kept(source)
        totals[p] = got[source] if totals[p] is None else totals[p] + got[source]
    everywhere = totals[0] + totals[1] + totals[2] + totals[3]
    for i in range(planes):
        density[i] = everywhere[i : i + 1]
        for c in range(3):
            current[c, i] = totals[i][planes + c : planes + c + 1]


def body(orbitals, potential, laser_field, box_anchor, domain_atoms, projector, strength):
    planes, rows, cells = orbitals.shape[2:]
    size = planes * rows
    domains = lax.axis_size("dom")
    orbs = lax.axis_size("orb")
    slots = domain_atoms.shape[1]
    me = lax.axis_index("dom")
    where = me.reshape(1).astype(jnp.int32)
    places = (where, domain_atoms, box_anchor)
    spot = (lax.axis_index("orb") // RUN).reshape(1).astype(jnp.int32)
    scale = 2.0 / orbs

    pairs = [(i, i ^ 1) for i in range(domains)]
    others = [(i, i + 1) for i in range(1, domains - 1, 2)] + [(i + 1, i) for i in range(1, domains - 1, 2)]

    def exchange(value):
        other = lax.ppermute(value, "dom", others)
        return other, lax.ppermute(value, "dom", pairs)

    def kernel(function, name, out, scalars, arrays, scratch):
        return pl.pallas_call(
            function,
            out_shape=out,
            in_specs=[SMEM] * scalars + [VMEM] * arrays,
            out_specs=jax.tree.map(lambda _: VMEM, out),
            scratch_shapes=scratch,
            compiler_params=pltpu.CompilerParams(vmem_limit_bytes=32 * 1024 * 1024),
            cost_estimate=pl.CostEstimate(flops=8_000_000, bytes_accessed=10_000_000, transcendentals=0),
            name=name,
        )

    sums = pltpu.VMEM((2 * slots * PROJ, cells), jnp.float32)
    u = orbitals.reshape(2, size, cells)
    proj, weight, first = kernel(
        functools.partial(prepare_kernel, planes, rows, slots),
        "prepare_real",
        (f32(PROJ * BOX, BOX, cells), f32(8, cells), f32(size + 8, cells)),
        4, 2, [sums],
    )(*places, strength, projector, u)
    v, second = kernel(
        functools.partial(second_kernel, planes, rows, slots, domains),
        "prepare_imag",
        (f32(planes, rows, cells), f32(size + 8, cells)),
        4, 3, [sums],
    )(*places, laser_field, potential, proj, u)

    def step(order, channel, halos, evolved, held=None):
        sign = 1.0 if (channel + order) % 2 == 0 else -1.0
        last = False if order < TERMS else ("both" if held is not None else True)
        out = (f32(size, cells),)
        if not last:
            out = (f32(size + 8, cells),) + out
        if last == "both":
            out = (f32(2, size, cells), f32(planes, rows, cells))
        padded = pltpu.VMEM((planes, rows + 16, cells), jnp.float32)
        extra = ()
        if held is not None:
            local = kernel(
                functools.partial(local_kernel, planes, rows), "local_part", f32(size, cells), 0, 2, [padded]
            )(halos[0], v)
            extra = (held, local)
        return kernel(
            functools.partial(step_kernel, planes, rows, slots, sign * time_step / order, last, scale),
            "taylor_step", out, 3, 7 + len(extra),
            [
                pltpu.VMEM((size, cells), jnp.float32),
                padded,
                pltpu.VMEM((2 * slots * PROJ, cells), jnp.float32),
                sums,
            ],
        )(*places, *halos, v, weight, proj, evolved, *extra)

    terms = [first, second]
    totals = [first, second]
    for order in range(1, TERMS + 1):
        halos = [(term, *exchange(term)) for term in terms]
        if order == 1:
            first_halos = (first, second, *halos[0][1:], *halos[1][1:])
        if order == 2:
            halo, spot = lax.optimization_barrier((halos[0][1], spot))
            halos[0] = (halos[0][0], halo, halos[0][2])
            half = f32(3 * planes // 2, rows, cells)
            keep, send = kernel(
                functools.partial(current_kernel, planes, rows, scale),
                "current_part", (half, half), 2, 6,
                [pltpu.VMEM((2, planes, rows + 16, cells), jnp.float32)],
            )(where, spot, *first_halos)
            got = lax.ppermute(send, "orb", [(i, (i // RUN ^ 1) * RUN + i % RUN) for i in range(orbs)])
        if order == 3:
            halo, spot = lax.optimization_barrier((halos[0][1], spot))
            halos[0] = (halos[0][0], halo, halos[0][2])
            quarter = f32(3 * planes // 4, rows, cells)
            keep, send = kernel(merge_kernel, "merge_current", (quarter, quarter), 1, 2, [])(spot, keep, got)
            got = lax.ppermute(send, "orb", [(i, (i // RUN ^ 2) * RUN + i % RUN) for i in range(orbs)])
        for channel in (0, 1):
            to = (channel + order) % 2
            if order < TERMS:
                terms[channel], totals[to] = step(order, channel, halos[channel], totals[to])
            elif channel == 0:
                (totals[to],) = step(order, channel, halos[channel], totals[to])
            else:
                evolved, density = step(order, channel, halos[channel], totals[to], totals[1 - to])

    fields = jnp.concatenate([density, keep + got], axis=0)
    fields = jnp.moveaxis(fields, 1, 0)
    fields = lax.all_to_all(fields, "orb", 0, 0, tiled=True)
    density, current = kernel(
        functools.partial(gather_kernel, planes),
        "sum_over_orb", (f32(planes, 1, cells), f32(3, planes, 1, cells)), 0, 1, [],
    )(fields)
    return evolved.reshape(orbitals.shape), density, current


def solution(mesh):
    in_specs = (P(None, "orb", "dom", None, None), P("dom", None, None), P(), P(), P(), P(), P())
    out_specs = (
        P(None, "orb", "dom", None, None),
        P("dom", "orb", None),
        P(None, "dom", "orb", None),
    )
    return jax.shard_map(body, mesh=mesh, in_specs=in_specs, out_specs=out_specs, check_vma=False)
```
